32 devices in a mesh: row: 8 (over z, y), col: 4 (over x, core).
Axes of the slice: x: 2, y: 2, z: 4, core: 2. Of those that a mesh axis runs over, the one named last changes fastest.
Arguments:
- feat_in: bfloat16 [256, 256, 256], P('row', 'col'), may hold values from -6 to 6
- conv_weight: bfloat16 [2304, 256], P('col'), may hold values from -0.125 to 0.125
- conv_bias: float32 [256], replicated, may hold values from -4 to 4
- proj_weight: bfloat16 [256, 768], replicated, may hold values from -0.375 to 0.375
- qkv_weight: bfloat16 [768, 2304], P('row'), may hold values from -2 to 2
- tissue: int32 [128, 128], P('row', 'col'), may hold values from 0 to 1, as said below
- phase: int32 [128, 128], P('row', 'col'), may hold values from 0 to 3, as said below
Outputs:
- attended: bfloat16 [128, 128, 768], P('row', 'col')
The draws below stay inside these ranges and needn't reach their ends.
Inputs may be any that keep to these rules, and one draw needn't show every extreme that they name: Within each column strip, phase is the token column plus an offset drawn for each token row, modulo 4. In each device's block of tokens, every phase holds at least one tissue token.
All inputs are finite; a program needn't handle non-finite values.
Results may differ from the reference program's by a relative error of at most 0.0065.
Values may be sent and summed in bfloat16 or wider, within the bound.
No kernel may reach another device: no remote copies, remote signals or barrier semaphores. Data moves between devices by JAX's collectives and lax.ppermute only.
A program may use at most 64 MiB of HBM per device.

```python
import jax
import jax.numpy as jnp
from jax import lax

C = 256
HEADS = 12
HD = 64
D = 768
DILATION_STEP = 4
LOCAL_ROWS = 16
LOCAL_COLUMNS = 32
GROUP = 1024
SLIDE_ROWS = 128
SLIDE_COLUMNS = 128
N_COL = 4


def draw_phase(key, part):
    strip_count = SLIDE_COLUMNS // LOCAL_COLUMNS
    row_offsets = jax.random.randint(jax.random.fold_in(key, 13), (SLIDE_ROWS, strip_count), 0, DILATION_STEP, dtype=jnp.int32)
    spread_rows = jnp.repeat(row_offsets, LOCAL_COLUMNS, axis=1)
    column_indices = jnp.arange(SLIDE_COLUMNS, dtype=jnp.int32)[None, :] % LOCAL_COLUMNS
    return ((column_indices + spread_rows) % DILATION_STEP).astype(jnp.int32)


def draw_tissue(key, part):
    band_count = SLIDE_ROWS // LOCAL_ROWS
    band_index = jnp.arange(SLIDE_ROWS, dtype=jnp.int32) // LOCAL_ROWS
    edge_dist = jnp.minimum(band_index, band_count - 1 - band_index)
    threshold = 10 + 170 * edge_dist // band_count
    random_ints = jax.random.randint(jax.random.fold_in(key, 11), (SLIDE_ROWS, SLIDE_COLUMNS), 0, 100, dtype=jnp.int32)
    row_positions = jnp.arange(SLIDE_ROWS, dtype=jnp.int32)[:, None]
    column_positions = jnp.arange(SLIDE_COLUMNS, dtype=jnp.int32)[None, :]
    forced_flags = (row_positions % LOCAL_ROWS == 0) & (column_positions % LOCAL_COLUMNS < DILATION_STEP)
    tissue_live = (random_ints < threshold[:, None]) | forced_flags
    return tissue_live.astype(jnp.int32)


def draw_qkv_weight(key, part):
    basic_draw = jax.random.normal(jax.random.fold_in(key, 3), (D, 3 * D), jnp.float32) * D ** (-0.5)
    return jnp.clip(basic_draw, -2.0, 2.0).astype(jnp.bfloat16)


def steps_of(stream_key, extent, cuts, smallest, top_value):
    def one(position, shards_of):
        heights = jax.random.uniform(jax.random.fold_in(jax.random.fold_in(stream_key, 6), position), (shards_of,), jnp.float32, smallest / len(cuts), top_value / len(cuts))
        return jnp.repeat(jnp.exp(heights), extent[position] // shards_of).reshape((-1,) + (1,) * (len(extent) - position - 1))

    factor_of = one(*cuts[0])
    for cut in cuts[1:]:
        factor_of = factor_of * one(*cut)
    return factor_of


def gaussian(rng, dims, deviation, bound, split=(), held_as=jnp.bfloat16):
    factor_of = steps_of(rng, dims, split, -0.22, 0.18) if split else 1.0
    values = jax.random.normal(rng, dims, jnp.float32) * deviation * factor_of
    return jnp.minimum(jnp.maximum(values, -bound), bound).astype(held_as)


def setup_inputs(seed: int = 0) -> dict:
    key_list = jax.random.split(jax.random.key(seed), 8)
    return {
        "feat_in": gaussian(key_list[0], (2 * SLIDE_ROWS, 2 * SLIDE_COLUMNS, C), 1.0, 6.0, ((0, 8), (1, 4))),
        "conv_weight": gaussian(key_list[1], (9 * C, C), (9 * C) ** -0.5, 0.125, ((0, 4),)),
        "conv_bias": gaussian(key_list[2], (C,), 0.7, 4.0, (), jnp.float32),
        "proj_weight": gaussian(key_list[3], (C, D), C ** -0.5, 0.375),
        "qkv_weight": draw_qkv_weight(jax.random.fold_in(key_list[7], 71), 0),
        "tissue": draw_tissue(jax.random.fold_in(key_list[7], 71), 0),
        "phase": draw_phase(jax.random.fold_in(key_list[7], 71), 0),
    }


def layer_norm(values):
    centred = values - lax.optimization_barrier(jnp.mean(values, axis=-1, keepdims=True))
    spread_rows = lax.optimization_barrier(jnp.mean(centred * centred, axis=-1, keepdims=True))
    return centred * lax.rsqrt(spread_rows + 1e-05)

def group_attention(operands):
    qkv_group, tissue_group = operands
    queries = qkv_group[:, :D].reshape(GROUP, HEADS, HD).astype(jnp.float32)
    keys_all = qkv_group[:, D:2 * D].reshape(GROUP, HEADS, HD).astype(jnp.float32)
    values_all = qkv_group[:, 2 * D:].reshape(GROUP, HEADS, HD).astype(jnp.float32)
    scores = jnp.einsum('qhd,khd->hqk', queries, keys_all) * HD ** (-0.5)
    allowed = (tissue_group > 0)[None, None, :]
    scores = jnp.where(allowed, scores, -1e+30)
    top_score = lax.optimization_barrier(jnp.max(scores, axis=-1, keepdims=True))
    weights = jnp.where(allowed, jnp.exp(scores - top_score), 0.0)
    denominator = lax.optimization_barrier(jnp.sum(weights, axis=-1))
    rounded = weights.astype(jnp.bfloat16).astype(jnp.float32)
    mixed_heads = jnp.einsum('hqk,khd->qhd', rounded, values_all) / jnp.transpose(denominator)[:, :, None]
    mixed_heads = mixed_heads * tissue_group.astype(jnp.float32)[:, None, None]
    return mixed_heads.reshape(GROUP, D).astype(jnp.bfloat16)

def reference(feat_in, conv_weight, conv_bias, proj_weight, qkv_weight, tissue, phase):
    padded = jnp.pad(feat_in, ((1, 0), (1, 0), (0, 0)))
    summed = jnp.zeros((SLIDE_ROWS * SLIDE_COLUMNS, C), jnp.float32)
    for row_tap in range(3):
        for col_tap in range(3):
            window = padded[row_tap:row_tap + 2 * SLIDE_ROWS - 1:2, col_tap:col_tap + 2 * SLIDE_COLUMNS - 1:2, :]
            offset = (3 * row_tap + col_tap) * C
            summed = summed + jnp.dot(window.reshape(SLIDE_ROWS * SLIDE_COLUMNS, C), conv_weight[offset:offset + C], preferred_element_type=jnp.float32)
    features = jax.nn.gelu(summed + conv_bias).astype(jnp.bfloat16)
    strip_feat = features.reshape(SLIDE_ROWS, N_COL, LOCAL_COLUMNS, C).transpose(1, 0, 2, 3).reshape(N_COL, SLIDE_ROWS * LOCAL_COLUMNS, C)
    segment_per_row = (jnp.arange(SLIDE_ROWS, dtype=jnp.int32) // (2 * DILATION_STEP * LOCAL_ROWS)).astype(jnp.int32)
    group_labels = (segment_per_row[:, None] * DILATION_STEP + phase).astype(jnp.int32)
    strip_group = group_labels.reshape(SLIDE_ROWS, N_COL, LOCAL_COLUMNS).transpose(1, 0, 2).reshape(N_COL, SLIDE_ROWS * LOCAL_COLUMNS)
    strip_tissue = tissue.reshape(SLIDE_ROWS, N_COL, LOCAL_COLUMNS).transpose(1, 0, 2).reshape(N_COL, SLIDE_ROWS * LOCAL_COLUMNS)

    def strip_output(operands):
        feat_strip, group_strip, tissue_strip = operands
        projected = jnp.dot(feat_strip, proj_weight, preferred_element_type=jnp.float32)
        tokens_bf = layer_norm(projected).astype(jnp.bfloat16)
        qkv_all = jnp.dot(tokens_bf, qkv_weight, preferred_element_type=jnp.float32).astype(jnp.bfloat16)
        ordering = jnp.argsort(group_strip, stable=True).astype(jnp.int32)
        sorted_qkv = qkv_all[ordering].reshape(-1, GROUP, 3 * D)
        sorted_tissue = tissue_strip[ordering].reshape(-1, GROUP)
        attended_sorted = lax.map(group_attention, (sorted_qkv, sorted_tissue))
        return jnp.zeros((SLIDE_ROWS * LOCAL_COLUMNS, D), jnp.bfloat16).at[ordering].set(attended_sorted.reshape(-1, D))
    strips = lax.map(strip_output, (strip_feat, strip_group, strip_tissue))
    return strips.reshape(N_COL, SLIDE_ROWS, LOCAL_COLUMNS, D).transpose(1, 0, 2, 3).reshape(SLIDE_ROWS, SLIDE_COLUMNS, D)
```

```python
import functools
import math

import jax
import jax.numpy as jnp
from jax import lax
from jax.experimental import pallas as pl
from jax.experimental.pallas import tpu as pltpu
from jax.sharding import PartitionSpec as P

HD = 64
PHASES = 4
SEGMENT = 8
QBLOCK = 32
LANES = 128
BF16 = jnp.bfloat16
F32 = jnp.float32
NT = (((1,), (1,)), ((), ()))
TN = (((0,), (0,)), ((), ()))
VMEM = pltpu.VMEM
ANY = pl.ANY


def dot(a, b, dims=None):
    if dims is None:
        return jnp.dot(a, b, preferred_element_type=F32)
    return lax.dot_general(a, b, dims, preferred_element_type=F32)


def flip(array, axis, bits):
    return lax.ppermute(array, axis, [(i, i ^ bits) for i in range(lax.axis_size(axis))])


def shifted(array, axis):
    return lax.ppermute(array, axis, [(i, i + 1) for i in range(lax.axis_size(axis) - 1)])


def cornered(array):
    rows, cols = lax.axis_size("row"), lax.axis_size("col")
    pairs = [
        (i * cols + j, (i + 1) * cols + j + 1) for i in range(rows - 1) for j in range(cols - 1)
    ]
    return lax.ppermute(array, ("row", "col"), pairs)


def call(kernel, out_shape, in_spaces, out_spaces, scratch, args, cost, name):
    return pl.pallas_call(
        kernel,
        out_shape=out_shape,
        in_specs=[pl.BlockSpec(memory_space=s) for s in in_spaces],
        out_specs=(
            tuple(pl.BlockSpec(memory_space=s) for s in out_spaces)
            if isinstance(out_spaces, tuple)
            else pl.BlockSpec(memory_space=out_spaces)
        ),
        scratch_shapes=scratch,
        compiler_params=pltpu.CompilerParams(vmem_limit_bytes=40 * 1024 * 1024),
        cost_estimate=pl.CostEstimate(flops=cost[0], bytes_accessed=cost[1], transcendentals=0),
        name=name,
    )(*args)


def widen_kernel(x_ref, cls_ref, z_ref, pos_ref, wide):
    rows, cols, channels = x_ref.shape
    half = cols // 2
    tokens = cls_ref.shape[1]
    bucket = tokens // PHASES

    def one_row(r, carry):
        for c in range(channels // LANES):
            wide[r, c, pl.ds(0, 8), :] = jnp.zeros((8, LANES), F32)
            wide[r, c, pl.ds(8, cols), :] = x_ref[r, :, c * LANES : (c + 1) * LANES].astype(F32)
            for b in range(3):
                spot = b * channels + c * LANES
                z_ref[r % 2, r // 2, :, spot : spot + LANES] = wide[
                    r, c, pl.ds(7 + b, half, stride=2), :
                ].astype(BF16)
        return carry

    lax.fori_loop(0, rows, one_row, 0, unroll=2)

    classes = lax.broadcasted_iota(jnp.int32, (16, tokens), 0)
    cls = jnp.broadcast_to(cls_ref[...], (16, tokens))
    member = (classes == cls).astype(F32)
    earlier = (
        lax.broadcasted_iota(jnp.int32, (tokens, tokens), 0)
        < lax.broadcasted_iota(jnp.int32, (tokens, tokens), 1)
    ).astype(F32)
    rank = dot(member.astype(BF16), earlier.astype(BF16))
    odd = lax.rem(classes, 2) == 1
    live_before = jnp.where(odd & (classes - 1 == cls), 1.0, 0.0)
    start = (classes // 2 * bucket).astype(F32) + jnp.sum(live_before, axis=1, keepdims=True)
    place = jnp.sum(member * (rank + start), axis=0, keepdims=True).astype(jnp.int32)
    pos_ref[...] = jnp.broadcast_to(place, pos_ref.shape)


def conv_kernel(
    z_ref, w0, w1, w2, w3, left_ref, up_ref, corner_ref, bias_ref, proj_ref, pos_ref,
    out_ref, weight, edge, sems,
):
    out_rows, out_cols, wide = z_ref.shape[1:]
    channels = wide // 3
    tokens = out_rows * out_cols
    shard = w0.shape[0]
    mine = lax.axis_index("col")
    copies = []
    for j, ref in enumerate((w0, w1, w2, w3)):
        spot = pl.multiple_of((mine ^ j) * shard, 64)
        copies.append(pltpu.make_async_copy(ref, weight.at[pl.ds(spot, shard)], sems.at[j]))
        copies[-1].start()
    in_rows = left_ref.shape[0]
    corner = jnp.broadcast_to(corner_ref[...].astype(F32), (8, channels))
    halves = range(channels // LANES)
    for c in halves:
        few = slice(c * LANES, (c + 1) * LANES)
        edge[0, c, pl.ds(0, 8), :] = corner[:, few]
        edge[0, c, pl.ds(8, in_rows), :] = left_ref[:, few].astype(F32)
        edge[1, c, pl.ds(0, 8), :] = jnp.zeros((8, LANES), F32)
        edge[1, c, pl.ds(8, 2 * out_cols), :] = up_ref[:, few].astype(F32)

    def every_second(side, first, count):
        parts = [edge[side, c, pl.ds(first, count, stride=2), :] for c in halves]
        return jnp.concatenate(parts, axis=1).astype(BF16)

    lefts = [every_second(0, 7 + a, out_rows) for a in range(3)]
    ups = [every_second(1, 7 + b, out_cols) for b in range(3)]
    for copy in copies:
        copy.wait()
    even = z_ref[0].reshape(tokens, wide)
    odd = z_ref[1].reshape(tokens, wide)
    acc = dot(even, weight[wide : 2 * wide]) + dot(odd, weight[2 * wide : 3 * wide])
    above = dot(odd[: tokens - out_cols], weight[:wide])
    top = dot(jnp.concatenate(ups, axis=1), weight[:wide])
    acc = acc + jnp.concatenate([top, above], axis=0)
    side = sum(dot(lefts[a], weight[a * wide : a * wide + channels]) for a in range(3))
    grid = acc.reshape(out_rows, out_cols, channels)
    first = lax.broadcasted_iota(jnp.int32, grid.shape, 1) == 0
    grid = grid + jnp.where(first, side[:, None, :], 0.0)
    pre = grid.reshape(tokens, channels) + bias_ref[...]
    features = jax.nn.gelu(pre).astype(BF16)
    projected = dot(features, proj_ref[...])
    centred = projected - jnp.mean(projected, axis=1, keepdims=True)
    spread = jnp.mean(centred * centred, axis=1, keepdims=True)
    scaled = (features.astype(F32) * lax.rsqrt(spread + 1e-05)).astype(BF16)
    chosen = (
        lax.broadcasted_iota(jnp.int32, (tokens, tokens), 0)
        == jnp.broadcast_to(pos_ref[0:1], (tokens, tokens))
    ).astype(F32)
    out_ref[...] = dot(chosen.astype(BF16), scaled).astype(BF16)


def merge_kernel(ordered, *refs):
    pieces, (proj_ref, out_ref) = refs[:SEGMENT], refs[SEGMENT:]
    depth = pieces[0].shape[0]
    mine = 0 if ordered else lax.rem(lax.axis_index("row"), SEGMENT)
    mean = jnp.mean(proj_ref[...].astype(F32), axis=0, keepdims=True)
    total = None
    for j, piece in enumerate(pieces):
        spot = pl.multiple_of((mine ^ j) * depth, 32)
        part = proj_ref[pl.ds(spot, depth), :].astype(F32) - mean
        high = part.astype(BF16)
        low = (part - high.astype(F32)).astype(BF16)
        term = dot(piece[...], high, TN) + dot(piece[...], low, TN)
        total = term if total is None else total + term
    out_ref[...] = total.astype(BF16)


def query_kernel(f_ref, m0, m1, m2, m3, q_ref, v_ref, merged, sems):
    shard = m0.shape[0]
    width = 4 * shard // 3
    heads = width // HD
    blocks = q_ref.shape[0]
    mine = lax.axis_index("col")
    copies = []
    for j, ref in enumerate((m0, m1, m2, m3)):
        spot = pl.multiple_of((mine ^ j) * shard, 64)
        copies.append(pltpu.make_async_copy(ref, merged.at[pl.ds(spot, shard)], sems.at[j]))
        copies[-1].start()
    for copy in copies:
        copy.wait()
    f = f_ref[...]
    factor = math.log2(math.e) / math.sqrt(HD)
    lanes = lax.broadcasted_iota(jnp.int32, (1, 2 * HD), 1)
    for pair in range(heads // 2):
        both = slice(pair * 2 * HD, (pair + 1) * 2 * HD)
        queries = dot(f, merged[both], NT).astype(BF16).astype(F32)
        keys = merged[width + pair * 2 * HD : width + (pair + 1) * 2 * HD]
        for h in range(2):
            one = jnp.where(lanes // HD == h, queries, 0.0).astype(BF16)
            wide = (dot(one, keys) * factor).astype(BF16)
            q_ref[:, 2 * pair + h] = wide.reshape(blocks, QBLOCK, wide.shape[1])
    v_ref[...] = merged[2 * width :]


def attend_kernel(counts_ref, q_ref, v_ref, pos_ref, live_ref, *refs):
    items, (out_ref, rows32, keys, mixed) = refs[:SEGMENT], refs[SEGMENT:]
    blocks, heads, qblock, channels = q_ref.shape
    tokens = items[0].shape[0]
    bucket = tokens // PHASES
    per_phase = blocks // PHASES
    group = SEGMENT * bucket
    mine = lax.rem(lax.axis_index("row"), SEGMENT)
    step = 256
    halves = range(channels // LANES)

    for p in range(PHASES):
        filled = 0
        for j in range(SEGMENT):
            for c in halves:
                rows32[c, pl.ds(filled, bucket), :] = items[j][
                    p * bucket : (p + 1) * bucket, c * LANES : (c + 1) * LANES
                ].astype(F32)
            filled = filled + counts_ref[mine ^ j, p]
        for c in halves:
            rows32[c, pl.ds(filled, step), :] = jnp.zeros((step, LANES), F32)
        own = counts_ref[mine, p]
        block_count = (own + qblock - 1) // qblock

        for width in range(step, group + 1, step):

            @pl.when((filled > width - step) & (filled <= width))
            def _():
                for c in halves:
                    keys[0:width, c * LANES : (c + 1) * LANES] = rows32[c, 0:width, :].astype(BF16)
                bias = jnp.where(
                    lax.broadcasted_iota(jnp.int32, (1, width), 1) < filled, 0.0, -1e30
                )

                def one_block(b, carry):
                    spot = p * per_phase + b
                    for part in range(3):
                        few = slice(part * heads // 3, (part + 1) * heads // 3)
                        q = q_ref[spot, few].reshape(heads // 3 * qblock, channels)
                        k = keys[0:width, :]
                        scores = dot(q, k, NT) + bias
                        weights = jnp.exp2(scores - jnp.max(scores, axis=1, keepdims=True))
                        total = jnp.sum(weights, axis=1, keepdims=True)
                        mix = dot(weights.astype(BF16), k) / total
                        mixed[spot, few] = mix.astype(BF16).reshape(heads // 3, qblock, channels)
                    return carry

                lax.fori_loop(0, block_count, one_block, 0)

        def no_block(b, carry):
            mixed[p * per_phase + b] = jnp.zeros((heads, qblock, channels), BF16)
            return carry

        lax.fori_loop(block_count, per_phase, no_block, 0)

    heads_out = []
    for h in range(heads):
        heads_out.append(
            dot(mixed[:, h].reshape(tokens, channels), v_ref[h * HD : (h + 1) * HD], NT)
        )
    ordered = jnp.concatenate(heads_out, axis=1).astype(BF16)
    chosen = (
        (
            lax.broadcasted_iota(jnp.int32, (tokens, tokens), 0)
            == jnp.broadcast_to(pos_ref[0:1], (tokens, tokens))
        )
        & (jnp.broadcast_to(live_ref[...], (tokens, tokens)) > 0)
    ).astype(F32)
    out_ref[...] = dot(chosen.astype(BF16), ordered, TN).astype(BF16)


def local(feat_in, conv_weight, conv_bias, proj_weight, qkv_weight, tissue, phase):
    in_rows, in_cols, channels = feat_in.shape
    out_rows, out_cols = in_rows // 2, in_cols // 2
    tokens = out_rows * out_cols
    row_count, col_count = lax.axis_size("row"), lax.axis_size("col")
    depth, out_width = qkv_weight.shape
    width = out_width // 3
    heads = width // HD
    share = out_width // col_count

    weight_x = flip(conv_weight, "col", 2)
    weight_core = flip(conv_weight, "col", 1)
    left = shifted(feat_in[:, in_cols - 1, :], "col")
    up = shifted(feat_in[in_rows - 1], "row")
    corner = cornered(feat_in[in_rows - 1, in_cols - 1 :, :])
    weight_far = flip(weight_x, "col", 1)

    qkv_mine = lax.dynamic_slice(
        qkv_weight, (0, lax.axis_index("col") * share), (depth, share)
    )
    ordered = row_count != SEGMENT
    if ordered:
        whole = lax.all_gather(qkv_mine, "row", axis=0, tiled=True)
        pieces = list(whole.reshape(SEGMENT, width // SEGMENT, share))
    else:
        z_pieces = [qkv_mine] + [flip(qkv_mine, "row", 2 * k) for k in (1, 2, 3)]
        y_pieces = flip(jnp.concatenate(z_pieces, axis=0), "row", 1)
        pieces = []
        for k in range(4):
            pieces += [z_pieces[k], y_pieces[k * depth : (k + 1) * depth]]

    live = tissue.reshape(1, tokens)
    cls = phase.reshape(1, tokens) * 2 + (1 - live)
    here = (phase[None] == jnp.arange(PHASES, dtype=jnp.int32)[:, None, None]) & (tissue[None] > 0)
    own_counts = jnp.sum(here.astype(jnp.int32), axis=(1, 2)).reshape(1, PHASES)
    groups = [
        [s * SEGMENT + i for i in range(SEGMENT)] for s in range(row_count // SEGMENT)
    ]
    counts = lax.all_gather(own_counts, "row", axis=0, tiled=True, axis_index_groups=groups)

    z, pos = call(
        widen_kernel,
        (
            jax.ShapeDtypeStruct((2, out_rows, out_cols, 3 * channels), BF16),
            jax.ShapeDtypeStruct((8, tokens), jnp.int32),
        ),
        [VMEM, VMEM],
        (VMEM, VMEM),
        [VMEM((in_rows, channels // LANES, in_cols + 8, LANES), F32)],
        (feat_in, cls),
        (1 << 24, 5 << 20),
        "widen",
    )
    mine = call(
        conv_kernel,
        jax.ShapeDtypeStruct((tokens, channels), BF16),
        [VMEM, ANY, ANY, ANY, ANY, VMEM, VMEM, VMEM, VMEM, VMEM, VMEM],
        VMEM,
        [
            VMEM((9 * channels, channels), BF16),
            VMEM((2, channels // LANES, in_cols + 8, LANES), F32),
            pltpu.SemaphoreType.DMA((4,)),
        ],
        (
            z, conv_weight, weight_core, weight_x, weight_far, left, up, corner,
            conv_bias.reshape(1, channels), proj_weight, pos,
        ),
        (1 << 30, 6 << 20),
        "conv",
    )

    z_items = [mine] + [flip(mine, "row", 2 * k) for k in (1, 2, 3)]
    items = []
    for item in z_items:
        items += [item, flip(item, "row", 1)]

    merged = call(
        functools.partial(merge_kernel, ordered),
        jax.ShapeDtypeStruct((share, channels), BF16),
        [VMEM] * (SEGMENT + 1),
        VMEM,
        [],
        (*pieces, proj_weight.T),
        (1 << 28, 2 << 20),
        "merge",
    )
    merged_x = flip(merged, "col", 2)
    merged_core = flip(merged, "col", 1)
    merged_far = flip(merged_x, "col", 1)
    blocks = tokens // QBLOCK
    queries, values = call(
        query_kernel,
        (
            jax.ShapeDtypeStruct((blocks, heads, QBLOCK, channels), BF16),
            jax.ShapeDtypeStruct((width, channels), BF16),
        ),
        [VMEM, ANY, ANY, ANY, ANY],
        (VMEM, VMEM),
        [VMEM((out_width, channels), BF16), pltpu.SemaphoreType.DMA((4,))],
        (mine, merged, merged_core, merged_x, merged_far),
        (1 << 30, 6 << 20),
        "queries",
    )
    group = SEGMENT * tokens // PHASES
    attended = call(
        attend_kernel,
        jax.ShapeDtypeStruct((tokens, width), BF16),
        [pltpu.SMEM] + [VMEM] * (4 + SEGMENT),
        VMEM,
        [
            VMEM((channels // LANES, group + 256, LANES), F32),
            VMEM((group, channels), BF16),
            VMEM((blocks, heads, QBLOCK, channels), BF16),
        ],
        (counts, queries, values, pos, live, *items),
        (4 << 30, 8 << 20),
        "attend",
    )
    return attended.reshape(out_rows, out_cols, width)


def solution(mesh):
    in_specs = (
        P("row", "col", None),
        P("col", None),
        P(),
        P(),
        P("row", None),
        P("row", "col"),
        P("row", "col"),
    )
    out_specs = P("row", "col", None)
    return jax.shard_map(local, mesh=mesh, in_specs=in_specs, out_specs=out_specs, check_vma=False)
```

```python
import functools
import math

import jax
import jax.numpy as jnp
from jax import lax
from jax.experimental import pallas as pl
from jax.experimental.pallas import tpu as pltpu
from jax.sharding import PartitionSpec as P

HD = 64
PHASES = 4
SEGMENT = 8
LANES = 128
BF16 = jnp.bfloat16
F32 = jnp.float32
NT = (((1,), (1,)), ((), ()))
TN = (((0,), (0,)), ((), ()))
VMEM = pltpu.VMEM
ANY = pl.ANY


def dot(a, b, dims=None):
    if dims is None:
        return jnp.dot(a, b, preferred_element_type=F32)
    return lax.dot_general(a, b, dims, preferred_element_type=F32)


def flip(array, axis, bits):
    return lax.ppermute(array, axis, [(i, i ^ bits) for i in range(lax.axis_size(axis))])


def shifted(array, axis):
    return lax.ppermute(array, axis, [(i, i + 1) for i in range(lax.axis_size(axis) - 1)])


HOPS = (1, 3, 0, 2)


def ring(array):
    pairs = []
    for i in range(lax.axis_size("row")):
        z, y = i % SEGMENT // 2, i % 2
        pairs.append((i, i // SEGMENT * SEGMENT + 2 * HOPS[z] + y))
    return lax.ppermute(array, "row", pairs)


def behind(z):
    found = [z]
    for _ in range(len(HOPS) - 1):
        z = found[-1]
        found.append(jnp.where(z == 0, 2, jnp.where(z == 1, 0, jnp.where(z == 2, 3, 1))))
    return found


def call(kernel, out_shape, in_spaces, out_spaces, scratch, args, name):
    return pl.pallas_call(
        kernel,
        out_shape=out_shape,
        in_specs=[pl.BlockSpec(memory_space=s) for s in in_spaces],
        out_specs=(
            tuple(pl.BlockSpec(memory_space=s) for s in out_spaces)
            if isinstance(out_spaces, tuple)
            else pl.BlockSpec(memory_space=out_spaces)
        ),
        scratch_shapes=scratch,
        compiler_params=pltpu.CompilerParams(vmem_limit_bytes=40 * 1024 * 1024),
        cost_estimate=pl.CostEstimate(flops=0, bytes_accessed=0, transcendentals=0),
        name=name,
    )(*args)


def prepare_kernel(
    x_ref, tissue_ref, phase_ref, left_ref, z_ref, sort_ref, back_ref, wide
):
    rows, cols, channels = x_ref.shape
    out_rows, out_cols = tissue_ref.shape
    half = cols // 2
    tokens = out_rows * out_cols
    bucket = tokens // PHASES
    left_ref[...] = x_ref[:, cols - 1, :]
    def one_row(r, carry):
        for c in range(channels // LANES):
            wide[r, c, pl.ds(0, 8), :] = jnp.zeros((8, LANES), F32)
            wide[r, c, pl.ds(8, cols), :] = x_ref[r, :, c * LANES : (c + 1) * LANES].astype(F32)
            for b in range(3):
                spot = b * channels + c * LANES
                z_ref[r % 2, r // 2, :, spot : spot + LANES] = wide[
                    r, c, pl.ds(7 + b, half, stride=2), :
                ].astype(BF16)
        return carry

    lax.fori_loop(0, rows, one_row, 0, unroll=2)

    def iota(shape, axis):
        return lax.broadcasted_iota(jnp.int32, shape, axis)

    labels = (phase_ref[...] * 2 + 1 - tissue_ref[...]).astype(F32).astype(BF16)
    spread = (iota((out_cols, tokens), 0) == lax.rem(iota((out_cols, tokens), 1), out_cols)).astype(F32)
    along = dot(labels, spread.astype(BF16))
    in_row = iota((out_rows, tokens), 0) == iota((out_rows, tokens), 1) // out_cols
    cls = jnp.sum(jnp.where(in_row, along, 0.0), axis=0, keepdims=True).astype(jnp.int32)
    classes = iota((16, tokens), 0)
    cls = jnp.broadcast_to(cls, (16, tokens))
    member = (classes == cls).astype(F32)
    earlier = (iota((tokens, tokens), 0) < iota((tokens, tokens), 1)).astype(F32)
    rank = dot(member.astype(BF16), earlier.astype(BF16))
    odd = lax.rem(classes, 2) == 1
    live_before = jnp.where(odd & (classes - 1 == cls), 1.0, 0.0)
    start = (classes // 2 * bucket).astype(F32) + jnp.sum(live_before, axis=1, keepdims=True)
    place = jnp.sum(member * (rank + start), axis=0, keepdims=True)
    place = jnp.broadcast_to(place, (LANES, tokens))
    sort_ref[...] = (
        iota((tokens, tokens), 0) == jnp.broadcast_to(place[0:1].astype(jnp.int32), (tokens, tokens))
    ).astype(F32).astype(BF16)
    column = place.T[:, 0:1].astype(jnp.int32)
    back_ref[...] = (iota((tokens, tokens), 1) == column).astype(F32).astype(BF16)


def conv_kernel(
    z_hbm, w0, w1, w2, w3, proj_hbm, sort_hbm, left_ref, up_ref, bias_ref,
    out_ref, z_ref, weight, proj_ref, sort_ref, edge, sems,
):
    out_rows, out_cols, wide = z_ref.shape[1:]
    channels = wide // 3
    tokens = out_rows * out_cols
    shard = w0.shape[0]
    mine = lax.axis_index("col")
    copies = [pltpu.make_async_copy(z_hbm, z_ref, sems.at[4])]
    for j, ref in enumerate((w0, w1, w2, w3)):
        spot = pl.multiple_of((mine ^ j) * shard, 64)
        copies.append(pltpu.make_async_copy(ref, weight.at[pl.ds(spot, shard)], sems.at[j]))
    later = [
        pltpu.make_async_copy(proj_hbm, proj_ref, sems.at[5]),
        pltpu.make_async_copy(sort_hbm, sort_ref, sems.at[6]),
    ]
    for copy in copies + later:
        copy.start()
    in_rows = left_ref.shape[0]
    corner = up_ref[0:16].astype(F32)
    halves = range(channels // LANES)
    for c in halves:
        few = slice(c * LANES, (c + 1) * LANES)
        edge[0, c, pl.ds(0, 8), :] = corner[8:16, few]
        edge[0, c, pl.ds(8, in_rows), :] = left_ref[:, few].astype(F32)
        edge[1, c, pl.ds(0, 8), :] = jnp.zeros((8, LANES), F32)
        edge[1, c, pl.ds(8, 2 * out_cols), :] = up_ref[16:, few].astype(F32)

    def every_second(side, first, count):
        parts = [edge[side, c, pl.ds(first, count, stride=2), :] for c in halves]
        return jnp.concatenate(parts, axis=1).astype(BF16)

    lefts = [every_second(0, 7 + a, out_rows) for a in range(3)]
    ups = [every_second(1, 7 + b, out_cols) for b in range(3)]
    for copy in copies:
        copy.wait()
    even = z_ref[0].reshape(tokens, wide)
    odd = z_ref[1].reshape(tokens, wide)
    acc = dot(even, weight[wide : 2 * wide]) + dot(odd, weight[2 * wide : 3 * wide])
    above = dot(odd[: tokens - out_cols], weight[:wide])
    top = dot(jnp.concatenate(ups, axis=1), weight[:wide])
    acc = acc + jnp.concatenate([top, above], axis=0)
    side = sum(dot(lefts[a], weight[a * wide : a * wide + channels]) for a in range(3))
    grid = acc.reshape(out_rows, out_cols, channels)
    first = lax.broadcasted_iota(jnp.int32, grid.shape, 1) == 0
    grid = grid + jnp.where(first, side[:, None, :], 0.0)
    pre = grid.reshape(tokens, channels) + bias_ref[...]
    features = jax.nn.gelu(pre).astype(BF16)
    for copy in later:
        copy.wait()
    projected = dot(features, proj_ref[...])
    centred = projected - jnp.mean(projected, axis=1, keepdims=True)
    spread = jnp.mean(centred * centred, axis=1, keepdims=True)
    scaled = (features.astype(F32) * lax.rsqrt(spread + 1e-05)).astype(BF16)
    out_ref[...] = dot(sort_ref[...], scaled).astype(BF16)


def merge_kernel(ordered, *refs):
    pieces, (proj_ref, out_ref, counts_ref) = refs[:-3], refs[-3:]
    share = out_ref.shape[0]
    depth, lanes = pieces[0].shape
    mine = lax.rem(lax.axis_index("row"), SEGMENT)
    if ordered:
        order = range(SEGMENT)
    else:
        order = [2 * z + lax.rem(mine, 2) for z in behind(mine // 2)]
    mean = jnp.mean(proj_ref[...].astype(F32), axis=0, keepdims=True)
    total = None
    for piece, j in zip(pieces, order):
        spot = pl.multiple_of(j * depth, 32)
        part = proj_ref[pl.ds(spot, depth), :].astype(F32) - mean
        high = part.astype(BF16)
        low = (part - high.astype(F32)).astype(BF16)
        term = dot(piece[...], high, TN) + dot(piece[...], low, TN)
        total = term if total is None else total + term
    out_ref[...] = total[:share].astype(out_ref.dtype)
    rows = [piece[0:16, lanes - LANES :].astype(F32)[0:1] for piece in pieces]
    rows += [jnp.zeros((16 - len(rows), LANES), F32)]
    counts_ref[...] = jnp.concatenate(rows, axis=0).astype(BF16)


def join_kernel(mine_ref, got_ref, my_counts, got_counts, out_ref, counts_ref):
    out_ref[...] = (mine_ref[...] + got_ref[...].astype(F32)).astype(BF16)
    a, b = my_counts[...].astype(F32), got_counts[...].astype(F32)
    rows = [side[k : k + 1] for k in range(SEGMENT // 2) for side in (a, b)]
    counts_ref[...] = jnp.concatenate(rows, axis=0).astype(jnp.int32)


def query_kernel(f_ref, m0, m1, m2, m3, q_ref, v_ref, merged, sems):
    shard = m0.shape[0]
    width = 4 * shard // 3
    heads = width // HD
    blocks, _, bucket, _ = q_ref.shape
    mine = lax.axis_index("col")
    copies = []
    for j, ref in enumerate((m0, m1, m2, m3)):
        spot = pl.multiple_of((mine ^ j) * shard, 64)
        copies.append(pltpu.make_async_copy(ref, merged.at[pl.ds(spot, shard)], sems.at[j]))
        copies[-1].start()
    for copy in copies:
        copy.wait()
    f = f_ref[...]
    factor = math.log2(math.e) / math.sqrt(HD)
    lanes = lax.broadcasted_iota(jnp.int32, (1, 2 * HD), 1)
    for pair in range(heads // 2):
        both = slice(pair * 2 * HD, (pair + 1) * 2 * HD)
        queries = dot(f, merged[both], NT).astype(BF16).astype(F32)
        keys = merged[width + pair * 2 * HD : width + (pair + 1) * 2 * HD]
        for h in range(2):
            one = jnp.where(lanes // HD == h, queries, 0.0).astype(BF16)
            wide = (dot(one, keys) * factor).astype(BF16)
            q_ref[:, 2 * pair + h] = wide.reshape(blocks, bucket, wide.shape[1])
    v_ref[...] = merged[2 * width :].astype(F32).T.astype(BF16)


def attend_kernel(spare, counts_ref, q_hbm, v_hbm, back_hbm, *refs):
    items = refs[:SEGMENT]
    out_ref, rows32, keys, keys_t, mixed, q_ref, v_ref, back_ref, sems = refs[SEGMENT:]
    phases, heads, bucket, channels = q_ref.shape
    tokens = phases * bucket
    group = SEGMENT * bucket
    halves = range(channels // LANES)
    parts = 6
    share = heads // parts
    copies = [
        pltpu.make_async_copy(a, b, sems.at[i])
        for i, (a, b) in enumerate(((q_hbm, q_ref), (v_hbm, v_ref), (back_hbm, back_ref)))
    ]
    for copy in copies:
        copy.start()
    fills = []
    for p in range(phases):
        filled = 0
        for j in range(SEGMENT):
            for c in halves:
                rows32[p, c, pl.ds(filled, bucket), :] = items[j][
                    p * bucket : (p + 1) * bucket, c * LANES : (c + 1) * LANES
                ].astype(F32)
            filled = filled + counts_ref[j, spare + p]
        for c in halves:
            rows32[p, c, pl.ds(filled, group // 2), :] = jnp.zeros((group // 2, LANES), F32)
        fills.append(filled)
    most = functools.reduce(jnp.maximum, fills)
    for copy in copies:
        copy.wait()
    for width in (group // 2, group):

        @pl.when((most > width - group // 2) & (most <= width))
        def _():
            for p in range(phases):
                if width == group:

                    @pl.when(fills[p] < group // 2)
                    def _(p=p):
                        for c in halves:
                            rows32[p, c, group // 2 : group, :] = jnp.zeros((group // 2, LANES), F32)

                for c in halves:
                    some = rows32[p, c, 0:width, :]
                    keys[p, 0:width, c * LANES : (c + 1) * LANES] = some.astype(BF16)
                    keys_t[p, c * LANES : (c + 1) * LANES, 0:width] = some.T.astype(BF16)
                bias = jnp.where(
                    lax.broadcasted_iota(jnp.int32, (1, width), 1) < fills[p], 0.0, -1e30
                )
                for part in range(parts):
                    few = slice(part * share, (part + 1) * share)
                    q = q_ref[p, few].reshape(share * bucket, channels)
                    scores = dot(q, keys_t[p, :, 0:width]) + bias
                    weights = jnp.exp2(scores - jnp.max(scores, axis=1, keepdims=True))
                    total = jnp.sum(weights, axis=1, keepdims=True)
                    mix = dot(weights.astype(BF16), keys[p, 0:width, :]) * (1.0 / total)
                    mixed[p, few] = mix.astype(BF16).reshape(share, bucket, channels)

    outs = []
    lane = lax.broadcasted_iota(jnp.int32, (1, LANES), 1)
    for pair in range(heads // 2):
        some = v_ref[:, pair * LANES : (pair + 1) * LANES]
        a = dot(mixed[:, 2 * pair].reshape(tokens, channels), some)
        b = dot(mixed[:, 2 * pair + 1].reshape(tokens, channels), some)
        outs.append(jnp.where(lane < HD, a, b))
    spot = lax.broadcasted_iota(jnp.int32, (bucket, 1), 0)
    live = jnp.concatenate([spot < counts_ref[0, spare + p] for p in range(phases)], axis=0)
    ordered = jnp.where(live, jnp.concatenate(outs, axis=1), 0.0).astype(BF16)
    out_ref[...] = dot(back_ref[...], ordered).astype(BF16)


def local(feat_in, conv_weight, conv_bias, proj_weight, qkv_weight, tissue, phase):
    in_rows, in_cols, channels = feat_in.shape
    out_rows, out_cols = in_rows // 2, in_cols // 2
    tokens = out_rows * out_cols
    row_count, col_count = lax.axis_size("row"), lax.axis_size("col")
    depth, out_width = qkv_weight.shape
    width = out_width // 3
    heads = width // HD
    share = out_width // col_count

    weight_x = flip(conv_weight, "col", 2)
    weight_core = flip(conv_weight, "col", 1)
    weight_far = flip(weight_x, "col", 1)
    left, z, sort, back = call(
        prepare_kernel,
        (
            jax.ShapeDtypeStruct((in_rows, channels), BF16),
            jax.ShapeDtypeStruct((2, out_rows, out_cols, 3 * channels), BF16),
            jax.ShapeDtypeStruct((tokens, tokens), BF16),
            jax.ShapeDtypeStruct((tokens, tokens), BF16),
        ),
        [VMEM] * 3,
        (VMEM,) * 4,
        [VMEM((in_rows, channels // LANES, in_cols + 8, LANES), F32)],
        (feat_in, tissue, phase),
        "prepare",
    )
    left = shifted(left, "col")
    up = shifted(jnp.concatenate([left[in_rows - 16 :], feat_in[in_rows - 1]], axis=0), "row")

    here = (phase[None] == jnp.arange(PHASES, dtype=jnp.int32)[:, None, None]) & (tissue[None] > 0)
    own_counts = jnp.sum(here.astype(F32), axis=(1, 2)).astype(BF16)
    qkv_mine = lax.dynamic_slice(
        qkv_weight, (0, lax.axis_index("col") * share), (depth, share)
    )
    lanes = -share % LANES
    if lanes < PHASES:
        lanes += LANES
    beside = jnp.broadcast_to(jnp.pad(own_counts, (0, lanes - PHASES))[None], (depth, lanes))
    qkv_mine = jnp.concatenate([qkv_mine, beside], axis=1)
    spare = share % LANES
    ordered = row_count != SEGMENT
    if ordered:
        whole = lax.all_gather(qkv_mine, "row", axis=0, tiled=True)
        pieces = list(whole.reshape(SEGMENT, width // SEGMENT, share + lanes))
        groups = [
            [s * SEGMENT + i for i in range(SEGMENT)] for s in range(row_count // SEGMENT)
        ]
        spot = lax.rem(lax.axis_index("row"), SEGMENT)
        y = lax.rem(spot, 2)
        order = jnp.stack([2 * z_from + side for z_from in behind(spot // 2) for side in (y, 1 - y)])
        counts = lax.all_gather(own_counts, "row", axis_index_groups=groups)[order]
        counts = jnp.pad(counts.astype(jnp.int32), ((0, 0), (spare, LANES - spare - PHASES)))
    else:
        pieces = [qkv_mine]
        for _ in range(3):
            pieces.append(ring(pieces[-1]))
        z, *pieces = lax.optimization_barrier((z, *pieces))

    mine = call(
        conv_kernel,
        jax.ShapeDtypeStruct((tokens, channels), BF16),
        [ANY] * 7 + [VMEM] * 3,
        VMEM,
        [
            VMEM(z.shape, BF16),
            VMEM((9 * channels, channels), BF16),
            VMEM(proj_weight.shape, BF16),
            VMEM((tokens, tokens), BF16),
            VMEM((2, channels // LANES, in_cols + 8, LANES), F32),
            pltpu.SemaphoreType.DMA((7,)),
        ],
        (
            z, conv_weight, weight_core, weight_x, weight_far, proj_weight, sort, left, up,
            conv_bias.reshape(1, channels),
        ),
        "conv",
    )

    items = []
    item = mine
    for step in range(4):
        if step < 3:
            later, beside = ring(item), flip(item, "row", 1)
            later, beside = lax.optimization_barrier((later, beside))
        else:
            later, beside = None, flip(item, "row", 1)
        items += [item, beside]
        item = later

    merged, counts_mine = call(
        functools.partial(merge_kernel, ordered),
        (
            jax.ShapeDtypeStruct((share, channels), BF16 if ordered else F32),
            jax.ShapeDtypeStruct((16, LANES), BF16),
        ),
        [VMEM] * (len(pieces) + 1),
        (VMEM, VMEM),
        [],
        (*pieces, proj_weight.T),
        "merge",
    )
    if not ordered:
        got = flip(jnp.concatenate([merged.astype(BF16), jnp.pad(counts_mine, ((0, 0), (0, channels - LANES)))], axis=0), "row", 1)
        merged, counts = call(
            join_kernel,
            (
                jax.ShapeDtypeStruct((share, channels), BF16),
                jax.ShapeDtypeStruct((SEGMENT, LANES), jnp.int32),
            ),
            [VMEM] * 4,
            (VMEM, VMEM),
            [],
            (merged, got[:share], counts_mine, got[share:, :LANES]),
            "join",
        )
    merged_x = flip(merged, "col", 2)
    merged_core = flip(merged, "col", 1)
    merged_far = flip(merged_x, "col", 1)
    bucket = tokens // PHASES
    queries, values = call(
        query_kernel,
        (
            jax.ShapeDtypeStruct((PHASES, heads, bucket, channels), BF16),
            jax.ShapeDtypeStruct((channels, width), BF16),
        ),
        [VMEM, ANY, ANY, ANY, ANY],
        (VMEM, VMEM),
        [VMEM((out_width, channels), BF16), pltpu.SemaphoreType.DMA((4,))],
        (mine, merged, merged_core, merged_x, merged_far),
        "queries",
    )
    group = SEGMENT * bucket
    attended = call(
        functools.partial(attend_kernel, spare),
        jax.ShapeDtypeStruct((tokens, width), BF16),
        [pltpu.SMEM, ANY, ANY, ANY] + [VMEM] * SEGMENT,
        VMEM,
        [
            VMEM((PHASES, channels // LANES, group + group // 2, LANES), F32),
            VMEM((PHASES, group, channels), BF16),
            VMEM((PHASES, channels, group), BF16),
            VMEM(queries.shape, BF16),
            VMEM(queries.shape, BF16),
            VMEM(values.shape, BF16),
            VMEM((tokens, tokens), BF16),
            pltpu.SemaphoreType.DMA((3,)),
        ],
        (counts, queries, values, back, *items),
        "attend",
    )
    return attended.reshape(out_rows, out_cols, width)


def solution(mesh):
    in_specs = (
        P("row", "col", None),
        P("col", None),
        P(),
        P(),
        P("row", None),
        P("row", "col"),
        P("row", "col"),
    )
    out_specs = P("row", "col", None)
    return jax.shard_map(local, mesh=mesh, in_specs=in_specs, out_specs=out_specs, check_vma=False)
```

```python
import functools
import math

import jax
import jax.numpy as jnp
from jax import lax
from jax.experimental import pallas as pl
from jax.experimental.pallas import tpu as pltpu
from jax.sharding import PartitionSpec as P

HD = 64
PHASES = 4
SEGMENT = 8
LANES = 128
BF16 = jnp.bfloat16
F32 = jnp.float32
NT = (((1,), (1,)), ((), ()))
TN = (((0,), (0,)), ((), ()))
VMEM = pltpu.VMEM
ANY = pl.ANY


def dot(a, b, dims=None):
    if dims is None:
        return jnp.dot(a, b, preferred_element_type=F32)
    return lax.dot_general(a, b, dims, preferred_element_type=F32)


def flip(array, axis, bits):
    return lax.ppermute(array, axis, [(i, i ^ bits) for i in range(lax.axis_size(axis))])


def shifted(array, axis):
    return lax.ppermute(array, axis, [(i, i + 1) for i in range(lax.axis_size(axis) - 1)])


HOPS = (1, 3, 0, 2)


def ring(array):
    pairs = []
    for i in range(lax.axis_size("row")):
        z, y = i % SEGMENT // 2, i % 2
        pairs.append((i, i // SEGMENT * SEGMENT + 2 * HOPS[z] + y))
    return lax.ppermute(array, "row", pairs)


def behind(z):
    found = [z]
    for _ in range(len(HOPS) - 1):
        z = found[-1]
        found.append(jnp.where(z == 0, 2, jnp.where(z == 1, 0, jnp.where(z == 2, 3, 1))))
    return found


def call(kernel, out_shape, in_spaces, out_spaces, scratch, args, name, mib):
    return pl.pallas_call(
        kernel,
        out_shape=out_shape,
        in_specs=[pl.BlockSpec(memory_space=s) for s in in_spaces],
        out_specs=(
            tuple(pl.BlockSpec(memory_space=s) for s in out_spaces)
            if isinstance(out_spaces, tuple)
            else pl.BlockSpec(memory_space=out_spaces)
        ),
        scratch_shapes=scratch,
        compiler_params=pltpu.CompilerParams(vmem_limit_bytes=mib * 1024 * 1024),
        cost_estimate=pl.CostEstimate(flops=0, bytes_accessed=0, transcendentals=0),
        name=name,
    )(*args)


def prepare_kernel(
    x_ref, label_ref, left_ref, z_ref, sort_ref, back_ref, wide
):
    rows, cols, channels = x_ref.shape
    out_rows, out_cols = label_ref.shape
    half = cols // 2
    tokens = out_rows * out_cols
    bucket = tokens // PHASES
    left_ref[...] = x_ref[:, cols - 1, :]
    def one_row(r, carry):
        for c in range(channels // LANES):
            wide[r, c, pl.ds(0, 8), :] = jnp.zeros((8, LANES), F32)
            wide[r, c, pl.ds(8, cols), :] = x_ref[r, :, c * LANES : (c + 1) * LANES].astype(F32)
            for b in range(3):
                spot = b * channels + c * LANES
                z_ref[r % 2, r // 2, :, spot : spot + LANES] = wide[
                    r, c, pl.ds(7 + b, half, stride=2), :
                ].astype(BF16)
        return carry

    lax.fori_loop(0, rows, one_row, 0, unroll=2)

    def iota(shape, axis):
        return lax.broadcasted_iota(jnp.int32, shape, axis)

    labels = label_ref[...].astype(BF16)
    spread = (iota((out_cols, tokens), 0) == lax.rem(iota((out_cols, tokens), 1), out_cols)).astype(F32)
    along = dot(labels, spread.astype(BF16))
    in_row = iota((out_rows, tokens), 0) == iota((out_rows, tokens), 1) // out_cols
    cls = jnp.sum(jnp.where(in_row, along, 0.0), axis=0, keepdims=True).astype(jnp.int32)
    classes = iota((16, tokens), 0)
    cls = jnp.broadcast_to(cls, (16, tokens))
    member = (classes == cls).astype(F32)
    earlier = (iota((tokens, tokens), 0) < iota((tokens, tokens), 1)).astype(F32)
    rank = dot(member.astype(BF16), earlier.astype(BF16))
    odd = lax.rem(classes, 2) == 1
    live_before = jnp.where(odd & (classes - 1 == cls), 1.0, 0.0)
    start = (classes // 2 * bucket).astype(F32) + jnp.sum(live_before, axis=1, keepdims=True)
    place = jnp.sum(member * (rank + start), axis=0, keepdims=True)
    place = jnp.broadcast_to(place, (LANES, tokens))
    sort_ref[...] = (
        iota((tokens, tokens), 0) == jnp.broadcast_to(place[0:1].astype(jnp.int32), (tokens, tokens))
    ).astype(F32).astype(BF16)
    column = place.T[:, 0:1].astype(jnp.int32)
    back_ref[...] = (iota((tokens, tokens), 1) == column).astype(F32).astype(BF16)


def conv_kernel(
    z_hbm, w0, w1, w2, w3, proj_hbm, sort_hbm, left_ref, up_ref, bias_ref,
    out_ref, z_ref, weight, proj_ref, sort_ref, edge, sems,
):
    out_rows, out_cols, wide = z_ref.shape[1:]
    channels = wide // 3
    tokens = out_rows * out_cols
    shard = w0.shape[0]
    mine = lax.axis_index("col")
    copies = [pltpu.make_async_copy(z_hbm, z_ref, sems.at[4])]
    for j, ref in enumerate((w0, w1, w2, w3)):
        spot = pl.multiple_of((mine ^ j) * shard, 64)
        copies.append(pltpu.make_async_copy(ref, weight.at[pl.ds(spot, shard)], sems.at[j]))
    later = [
        pltpu.make_async_copy(proj_hbm, proj_ref, sems.at[5]),
        pltpu.make_async_copy(sort_hbm, sort_ref, sems.at[6]),
    ]
    for copy in copies + later:
        copy.start()
    in_rows = left_ref.shape[0]
    corner = up_ref[0:16].astype(F32)
    halves = range(channels // LANES)
    for c in halves:
        few = slice(c * LANES, (c + 1) * LANES)
        edge[0, c, pl.ds(0, 8), :] = corner[8:16, few]
        edge[0, c, pl.ds(8, in_rows), :] = left_ref[:, few].astype(F32)
        edge[1, c, pl.ds(0, 8), :] = jnp.zeros((8, LANES), F32)
        edge[1, c, pl.ds(8, 2 * out_cols), :] = up_ref[16:, few].astype(F32)

    def every_second(side, first, count):
        parts = [edge[side, c, pl.ds(first, count, stride=2), :] for c in halves]
        return jnp.concatenate(parts, axis=1).astype(BF16)

    lefts = [every_second(0, 7 + a, out_rows) for a in range(3)]
    ups = [every_second(1, 7 + b, out_cols) for b in range(3)]
    for copy in copies:
        copy.wait()
    even = z_ref[0].reshape(tokens, wide)
    odd = z_ref[1].reshape(tokens, wide)
    acc = dot(even, weight[wide : 2 * wide]) + dot(odd, weight[2 * wide : 3 * wide])
    above = dot(odd[: tokens - out_cols], weight[:wide])
    top = dot(jnp.concatenate(ups, axis=1), weight[:wide])
    acc = acc + jnp.concatenate([top, above], axis=0)
    side = sum(dot(lefts[a], weight[a * wide : a * wide + channels]) for a in range(3))
    grid = acc.reshape(out_rows, out_cols, channels)
    first = lax.broadcasted_iota(jnp.int32, grid.shape, 1) == 0
    grid = grid + jnp.where(first, side[:, None, :], 0.0)
    pre = grid.reshape(tokens, channels) + bias_ref[...]
    features = jax.nn.gelu(pre).astype(BF16)
    for copy in later:
        copy.wait()
    projected = dot(features, proj_ref[...])
    centred = projected - jnp.mean(projected, axis=1, keepdims=True)
    spread = jnp.mean(centred * centred, axis=1, keepdims=True)
    scaled = (features.astype(F32) * lax.rsqrt(spread + 1e-05)).astype(BF16)
    out_ref[...] = dot(sort_ref[...], scaled).astype(BF16)


def merge_kernel(ordered, *refs):
    pieces, (proj_ref, out_ref, counts_ref) = refs[:-3], refs[-3:]
    share = out_ref.shape[0]
    depth, lanes = pieces[0].shape
    mine = lax.rem(lax.axis_index("row"), SEGMENT)
    if ordered:
        order = range(SEGMENT)
    else:
        order = [2 * z + lax.rem(mine, 2) for z in behind(mine // 2)]
    mean = jnp.mean(proj_ref[...].astype(F32), axis=0, keepdims=True)
    total = None
    for piece, j in zip(pieces, order):
        spot = pl.multiple_of(j * depth, 32)
        part = proj_ref[pl.ds(spot, depth), :].astype(F32) - mean
        high = part.astype(BF16)
        low = (part - high.astype(F32)).astype(BF16)
        term = dot(piece[...], high, TN) + dot(piece[...], low, TN)
        total = term if total is None else total + term
    out_ref[...] = total[:share].astype(out_ref.dtype)
    rows = [piece[0:16, lanes - LANES :].astype(F32)[0:1] for piece in pieces]
    rows += [jnp.zeros((16 - len(rows), LANES), F32)]
    counts_ref[...] = jnp.concatenate(rows, axis=0).astype(BF16)


def join_kernel(mine_ref, got_ref, my_counts, got_counts, out_ref, counts_ref):
    out_ref[...] = (mine_ref[...] + got_ref[...].astype(F32)).astype(BF16)
    a, b = my_counts[...].astype(F32), got_counts[...].astype(F32)
    rows = [side[k : k + 1] for k in range(SEGMENT // 2) for side in (a, b)]
    counts_ref[...] = jnp.concatenate(rows, axis=0).astype(jnp.int32)


def query_kernel(f_ref, m0, m1, m2, m3, q_ref, v_ref, merged, sems):
    shard = m0.shape[0]
    width = 4 * shard // 3
    heads = width // HD
    blocks, _, bucket, _ = q_ref.shape
    mine = lax.axis_index("col")
    copies = []
    for j, ref in enumerate((m0, m1, m2, m3)):
        spot = pl.multiple_of((mine ^ j) * shard, 64)
        copies.append(pltpu.make_async_copy(ref, merged.at[pl.ds(spot, shard)], sems.at[j]))
        copies[-1].start()
    for copy in copies:
        copy.wait()
    f = f_ref[...]
    factor = math.log2(math.e) / math.sqrt(HD)
    lanes = lax.broadcasted_iota(jnp.int32, (1, 2 * HD), 1)
    for pair in range(heads // 2):
        both = slice(pair * 2 * HD, (pair + 1) * 2 * HD)
        queries = dot(f, merged[both], NT).astype(BF16).astype(F32)
        keys = merged[width + pair * 2 * HD : width + (pair + 1) * 2 * HD]
        for h in range(2):
            one = jnp.where(lanes // HD == h, queries, 0.0).astype(BF16)
            wide = (dot(one, keys) * factor).astype(BF16)
            q_ref[:, 2 * pair + h] = wide.reshape(blocks, bucket, wide.shape[1])
    v_ref[...] = merged[2 * width :].astype(F32).T.astype(BF16)


def attend_kernel(spare, counts_ref, q_hbm, v_hbm, back_hbm, *refs):
    around, across = refs[:4], refs[4:8]
    out_ref, rows32, keys, keys_t, mixed, q_ref, v_ref, back_ref, sems = refs[8:]
    phases, heads, bucket, channels = q_ref.shape
    tokens = phases * bucket
    group = SEGMENT * bucket

    def part_of(j, p):
        step, side = j // 2, j % 2
        if side == 0:
            return around[step], p * bucket
        if step != 1 or 2 * p < phases:
            return across[step], p * bucket
        return around[2], tokens + (2 * p - phases) * bucket // 2

    halves = range(channels // LANES)
    parts = 6
    share = heads // parts
    copies = [
        pltpu.make_async_copy(a, b, sems.at[i])
        for i, (a, b) in enumerate(((q_hbm, q_ref), (v_hbm, v_ref), (back_hbm, back_ref)))
    ]
    for copy in copies:
        copy.start()
    fills = []
    for p in range(phases):
        filled = 0
        for j in range(SEGMENT):
            source, first = part_of(j, p)
            for c in halves:
                rows32[p, c, pl.ds(filled, bucket), :] = source[
                    first : first + bucket, c * LANES : (c + 1) * LANES
                ].astype(F32)
            filled = filled + counts_ref[j, spare + p]
        for c in halves:
            rows32[p, c, pl.ds(filled, group // 2), :] = jnp.zeros((group // 2, LANES), F32)
        fills.append(filled)
    most = functools.reduce(jnp.maximum, fills)
    for copy in copies:
        copy.wait()
    for width in (group // 2, group):

        @pl.when((most > width - group // 2) & (most <= width))
        def _():
            for p in range(phases):
                if width == group:

                    @pl.when(fills[p] < group // 2)
                    def _(p=p):
                        for c in halves:
                            rows32[p, c, group // 2 : group, :] = jnp.zeros((group // 2, LANES), F32)

                for c in halves:
                    some = rows32[p, c, 0:width, :]
                    keys[p, 0:width, c * LANES : (c + 1) * LANES] = some.astype(BF16)
                    keys_t[p, c * LANES : (c + 1) * LANES, 0:width] = some.T.astype(BF16)
                bias = jnp.where(
                    lax.broadcasted_iota(jnp.int32, (1, width), 1) < fills[p], 0.0, -1e30
                )
                for part in range(parts):
                    few = slice(part * share, (part + 1) * share)
                    q = q_ref[p, few].reshape(share * bucket, channels)
                    scores = dot(q, keys_t[p, :, 0:width]) + bias
                    weights = jnp.exp2(scores - jnp.max(scores, axis=1, keepdims=True))
                    total = jnp.sum(weights, axis=1, keepdims=True)
                    mix = dot(weights.astype(BF16), keys[p, 0:width, :]) * (1.0 / total)
                    mixed[p, few] = mix.astype(BF16).reshape(share, bucket, channels)

    outs = []
    lane = lax.broadcasted_iota(jnp.int32, (1, LANES), 1)
    for pair in range(heads // 2):
        some = v_ref[:, pair * LANES : (pair + 1) * LANES]
        a = dot(mixed[:, 2 * pair].reshape(tokens, channels), some)
        b = dot(mixed[:, 2 * pair + 1].reshape(tokens, channels), some)
        outs.append(jnp.where(lane < HD, a, b))
    spot = lax.broadcasted_iota(jnp.int32, (bucket, 1), 0)
    live = jnp.concatenate([spot < counts_ref[0, spare + p] for p in range(phases)], axis=0)
    ordered = jnp.where(live, jnp.concatenate(outs, axis=1), 0.0).astype(BF16)
    out_ref[...] = dot(back_ref[...], ordered).astype(BF16)


def local(feat_in, conv_weight, conv_bias, proj_weight, qkv_weight, tissue, phase):
    in_rows, in_cols, channels = feat_in.shape
    out_rows, out_cols = in_rows // 2, in_cols // 2
    tokens = out_rows * out_cols
    row_count, col_count = lax.axis_size("row"), lax.axis_size("col")
    depth, out_width = qkv_weight.shape
    width = out_width // 3
    heads = width // HD
    share = out_width // col_count

    weight_x = flip(conv_weight, "col", 2)
    weight_core = flip(conv_weight, "col", 1)
    weight_far = flip(weight_x, "col", 1)
    labels = (phase * 2 + 1 - tissue).astype(F32)
    left, z, sort, back = call(
        prepare_kernel,
        (
            jax.ShapeDtypeStruct((in_rows, channels), BF16),
            jax.ShapeDtypeStruct((2, out_rows, out_cols, 3 * channels), BF16),
            jax.ShapeDtypeStruct((tokens, tokens), BF16),
            jax.ShapeDtypeStruct((tokens, tokens), BF16),
        ),
        [VMEM] * 2,
        (VMEM,) * 4,
        [VMEM((in_rows, channels // LANES, in_cols + 8, LANES), F32)],
        (feat_in, labels),
        "prepare",
        24,
    )
    left = shifted(left, "col")
    up = shifted(jnp.concatenate([left[in_rows - 16 :], feat_in[in_rows - 1]], axis=0), "row")

    here = labels[None] == 2.0 * jnp.arange(PHASES, dtype=F32)[:, None, None]
    own_counts = jnp.sum(here.astype(F32), axis=(1, 2)).astype(BF16)
    qkv_mine = lax.dynamic_slice(
        qkv_weight, (0, lax.axis_index("col") * share), (depth, share)
    )
    lanes = -share % LANES
    if lanes < PHASES:
        lanes += LANES
    beside = jnp.broadcast_to(jnp.pad(own_counts, (0, lanes - PHASES))[None], (depth, lanes))
    qkv_mine = jnp.concatenate([qkv_mine, beside], axis=1)
    spare = share % LANES
    ordered = row_count != SEGMENT
    if ordered:
        whole = lax.all_gather(qkv_mine, "row", axis=0, tiled=True)
        pieces = list(whole.reshape(SEGMENT, width // SEGMENT, share + lanes))
        groups = [
            [s * SEGMENT + i for i in range(SEGMENT)] for s in range(row_count // SEGMENT)
        ]
        spot = lax.rem(lax.axis_index("row"), SEGMENT)
        y = lax.rem(spot, 2)
        order = jnp.stack([2 * z_from + side for z_from in behind(spot // 2) for side in (y, 1 - y)])
        counts = lax.all_gather(own_counts, "row", axis_index_groups=groups)[order]
        counts = jnp.pad(counts.astype(jnp.int32), ((0, 0), (spare, LANES - spare - PHASES)))
    else:
        pieces = [qkv_mine]
        for _ in range(3):
            pieces.append(ring(pieces[-1]))
        z, *pieces = lax.optimization_barrier((z, *pieces))

    mine = call(
        conv_kernel,
        jax.ShapeDtypeStruct((tokens, channels), BF16),
        [ANY] * 7 + [VMEM] * 3,
        VMEM,
        [
            VMEM(z.shape, BF16),
            VMEM((9 * channels, channels), BF16),
            VMEM(proj_weight.shape, BF16),
            VMEM((tokens, tokens), BF16),
            VMEM((2, channels // LANES, in_cols + 8, LANES), F32),
            pltpu.SemaphoreType.DMA((7,)),
        ],
        (
            z, conv_weight, weight_core, weight_x, weight_far, proj_weight, sort, left, up,
            conv_bias.reshape(1, channels),
        ),
        "conv",
        24,
    )

    half = tokens // 2
    around, across = [mine], []
    message = mine
    for step in range(4):
        passed = flip(message[:half] if step == 1 else message[:tokens], "row", 1)
        if step < 3:
            message, passed = lax.optimization_barrier((ring(message[:tokens] if step == 2 else message), passed))
            around.append(message)
        across.append(passed)
        if step == 0:
            message = jnp.concatenate([message, passed[half:]], axis=0)

    merged, counts_mine = call(
        functools.partial(merge_kernel, ordered),
        (
            jax.ShapeDtypeStruct((share, channels), BF16 if ordered else F32),
            jax.ShapeDtypeStruct((16, LANES), BF16),
        ),
        [VMEM] * (len(pieces) + 1),
        (VMEM, VMEM),
        [],
        (*pieces, proj_weight.T),
        "merge",
        16,
    )
    if not ordered:
        got = flip(jnp.concatenate([merged.astype(BF16), jnp.pad(counts_mine, ((0, 0), (0, channels - LANES)))], axis=0), "row", 1)
        merged, counts = call(
            join_kernel,
            (
                jax.ShapeDtypeStruct((share, channels), BF16),
                jax.ShapeDtypeStruct((SEGMENT, LANES), jnp.int32),
            ),
            [VMEM] * 4,
            (VMEM, VMEM),
            [],
            (merged, got[:share], counts_mine, got[share:, :LANES]),
            "join",
            16,
        )
    merged_x = flip(merged, "col", 2)
    merged_core = flip(merged, "col", 1)
    merged_far = flip(merged_x, "col", 1)
    bucket = tokens // PHASES
    queries, values = call(
        query_kernel,
        (
            jax.ShapeDtypeStruct((PHASES, heads, bucket, channels), BF16),
            jax.ShapeDtypeStruct((channels, width), BF16),
        ),
        [VMEM, ANY, ANY, ANY, ANY],
        (VMEM, VMEM),
        [VMEM((out_width, channels), BF16), pltpu.SemaphoreType.DMA((4,))],
        (mine, merged, merged_core, merged_x, merged_far),
        "queries",
        24,
    )
    group = SEGMENT * bucket
    attended = call(
        functools.partial(attend_kernel, spare),
        jax.ShapeDtypeStruct((tokens, width), BF16),
        [pltpu.SMEM, ANY, ANY, ANY] + [VMEM] * SEGMENT,
        VMEM,
        [
            VMEM((PHASES, channels // LANES, group + group // 2, LANES), F32),
            VMEM((PHASES, group, channels), BF16),
            VMEM((PHASES, channels, group), BF16),
            VMEM(queries.shape, BF16),
            VMEM(queries.shape, BF16),
            VMEM(values.shape, BF16),
            VMEM((tokens, tokens), BF16),
            pltpu.SemaphoreType.DMA((3,)),
        ],
        (counts, queries, values, back, *around, *across),
        "attend",
        36,
    )
    return attended.reshape(out_rows, out_cols, width)


def solution(mesh):
    in_specs = (
        P("row", "col", None),
        P("col", None),
        P(),
        P(),
        P("row", None),
        P("row", "col"),
        P("row", "col"),
    )
    out_specs = P("row", "col", None)
    return jax.shard_map(local, mesh=mesh, in_specs=in_specs, out_specs=out_specs, check_vma=False)
```

```python
import functools
import math

import jax
import jax.numpy as jnp
from jax import lax
from jax.experimental import pallas as pl
from jax.experimental.pallas import tpu as pltpu
from jax.sharding import PartitionSpec as P

HD = 64
PHASES = 4
SEGMENT = 8
LANES = 128
BF16 = jnp.bfloat16
F32 = jnp.float32
NT = (((1,), (1,)), ((), ()))
TN = (((0,), (0,)), ((), ()))
VMEM = pltpu.VMEM
ANY = pl.ANY


def dot(a, b, dims=None):
    if dims is None:
        return jnp.dot(a, b, preferred_element_type=F32)
    return lax.dot_general(a, b, dims, preferred_element_type=F32)


def flip(array, axis, bits):
    return lax.ppermute(array, axis, [(i, i ^ bits) for i in range(lax.axis_size(axis))])


def shifted(array, axis):
    return lax.ppermute(array, axis, [(i, i + 1) for i in range(lax.axis_size(axis) - 1)])


HOPS = (1, 3, 0, 2)


def ring(array):
    pairs = []
    for i in range(lax.axis_size("row")):
        z, y = i % SEGMENT // 2, i % 2
        pairs.append((i, i // SEGMENT * SEGMENT + 2 * HOPS[z] + y))
    return lax.ppermute(array, "row", pairs)


def behind(z):
    found = [z]
    for _ in range(len(HOPS) - 1):
        z = found[-1]
        found.append(jnp.where(z == 0, 2, jnp.where(z == 1, 0, jnp.where(z == 2, 3, 1))))
    return found


def call(kernel, out_shape, in_spaces, out_spaces, scratch, args, name, mib):
    return pl.pallas_call(
        kernel,
        out_shape=out_shape,
        in_specs=[pl.BlockSpec(memory_space=s) for s in in_spaces],
        out_specs=(
            tuple(pl.BlockSpec(memory_space=s) for s in out_spaces)
            if isinstance(out_spaces, tuple)
            else pl.BlockSpec(memory_space=out_spaces)
        ),
        scratch_shapes=scratch,
        compiler_params=pltpu.CompilerParams(vmem_limit_bytes=mib * 1024 * 1024),
        cost_estimate=pl.CostEstimate(flops=0, bytes_accessed=0, transcendentals=0),
        name=name,
    )(*args)


def prepare_kernel(
    x_ref, label_ref, left_ref, z_ref, sort_ref, back_ref, wide
):
    rows, cols, channels = x_ref.shape
    out_rows, out_cols = label_ref.shape
    half = cols // 2
    tokens = out_rows * out_cols
    bucket = tokens // PHASES
    left_ref[...] = x_ref[:, cols - 1, :]
    def one_row(r, carry):
        for c in range(channels // LANES):
            wide[r, c, pl.ds(0, 8), :] = jnp.zeros((8, LANES), F32)
            wide[r, c, pl.ds(8, cols), :] = x_ref[r, :, c * LANES : (c + 1) * LANES].astype(F32)
            for b in range(3):
                spot = b * channels + c * LANES
                z_ref[r % 2, r // 2, :, spot : spot + LANES] = wide[
                    r, c, pl.ds(7 + b, half, stride=2), :
                ].astype(BF16)
        return carry

    lax.fori_loop(0, rows, one_row, 0, unroll=2)

    def iota(shape, axis):
        return lax.broadcasted_iota(jnp.int32, shape, axis)

    labels = label_ref[...].astype(BF16)
    spread = (iota((out_cols, tokens), 0) == lax.rem(iota((out_cols, tokens), 1), out_cols)).astype(F32)
    along = dot(labels, spread.astype(BF16))
    in_row = iota((out_rows, tokens), 0) == iota((out_rows, tokens), 1) // out_cols
    cls = jnp.sum(jnp.where(in_row, along, 0.0), axis=0, keepdims=True).astype(jnp.int32)
    classes = iota((16, tokens), 0)
    cls = jnp.broadcast_to(cls, (16, tokens))
    member = (classes == cls).astype(F32)
    earlier = (iota((tokens, tokens), 0) < iota((tokens, tokens), 1)).astype(F32)
    rank = dot(member.astype(BF16), earlier.astype(BF16))
    odd = lax.rem(classes, 2) == 1
    live_before = jnp.where(odd & (classes - 1 == cls), 1.0, 0.0)
    start = (classes // 2 * bucket).astype(F32) + jnp.sum(live_before, axis=1, keepdims=True)
    place = jnp.sum(member * (rank + start), axis=0, keepdims=True)
    place = jnp.broadcast_to(place, (LANES, tokens))
    sort_ref[...] = (
        iota((tokens, tokens), 0) == jnp.broadcast_to(place[0:1].astype(jnp.int32), (tokens, tokens))
    ).astype(F32).astype(BF16)
    column = place.T[:, 0:1].astype(jnp.int32)
    back_ref[...] = (iota((tokens, tokens), 1) == column).astype(F32).astype(BF16)


def conv_kernel(
    z_ref, w0, w1, w2, w3, proj_ref, sort_ref, left_ref, up_ref, bias_ref,
    out_ref, weight, edge, sems,
):
    out_rows, out_cols, wide = z_ref.shape[1:]
    channels = wide // 3
    tokens = out_rows * out_cols
    shard = w0.shape[0]
    mine = lax.axis_index("col")
    copies = []
    for j, ref in enumerate((w0, w1, w2, w3)):
        spot = pl.multiple_of((mine ^ j) * shard, 64)
        copies.append(pltpu.make_async_copy(ref, weight.at[pl.ds(spot, shard)], sems.at[j]))
    for copy in copies:
        copy.start()
    in_rows = left_ref.shape[0]
    corner = up_ref[0:16].astype(F32)
    halves = range(channels // LANES)
    for c in halves:
        few = slice(c * LANES, (c + 1) * LANES)
        edge[0, c, pl.ds(0, 8), :] = corner[8:16, few]
        edge[0, c, pl.ds(8, in_rows), :] = left_ref[:, few].astype(F32)
        edge[1, c, pl.ds(0, 8), :] = jnp.zeros((8, LANES), F32)
        edge[1, c, pl.ds(8, 2 * out_cols), :] = up_ref[16:, few].astype(F32)

    def every_second(side, first, count):
        parts = [edge[side, c, pl.ds(first, count, stride=2), :] for c in halves]
        return jnp.concatenate(parts, axis=1).astype(BF16)

    lefts = [every_second(0, 7 + a, out_rows) for a in range(3)]
    ups = [every_second(1, 7 + b, out_cols) for b in range(3)]
    for copy in copies:
        copy.wait()
    even = z_ref[0].reshape(tokens, wide)
    odd = z_ref[1].reshape(tokens, wide)
    acc = dot(even, weight[wide : 2 * wide]) + dot(odd, weight[2 * wide : 3 * wide])
    above = dot(odd[: tokens - out_cols], weight[:wide])
    top = dot(jnp.concatenate(ups, axis=1), weight[:wide])
    acc = acc + jnp.concatenate([top, above], axis=0)
    side = sum(dot(lefts[a], weight[a * wide : a * wide + channels]) for a in range(3))
    grid = acc.reshape(out_rows, out_cols, channels)
    first = lax.broadcasted_iota(jnp.int32, grid.shape, 1) == 0
    grid = grid + jnp.where(first, side[:, None, :], 0.0)
    pre = grid.reshape(tokens, channels) + bias_ref[...]
    features = jax.nn.gelu(pre).astype(BF16)
    projected = dot(features, proj_ref[...])
    centred = projected - jnp.mean(projected, axis=1, keepdims=True)
    spread = jnp.mean(centred * centred, axis=1, keepdims=True)
    scaled = (features.astype(F32) * lax.rsqrt(spread + 1e-05)).astype(BF16)
    out_ref[...] = dot(sort_ref[...], scaled).astype(BF16)


def merge_kernel(ordered, *refs):
    pieces, (proj_ref, out_ref, counts_ref) = refs[:-3], refs[-3:]
    share = out_ref.shape[0]
    depth, lanes = pieces[0].shape
    mine = lax.rem(lax.axis_index("row"), SEGMENT)
    if ordered:
        order = range(SEGMENT)
    else:
        order = [2 * z + lax.rem(mine, 2) for z in behind(mine // 2)]
    mean = jnp.mean(proj_ref[...].astype(F32), axis=0, keepdims=True)
    total = None
    for piece, j in zip(pieces, order):
        spot = pl.multiple_of(j * depth, 32)
        part = proj_ref[pl.ds(spot, depth), :].astype(F32) - mean
        high = part.astype(BF16)
        low = (part - high.astype(F32)).astype(BF16)
        term = dot(piece[...], high, TN) + dot(piece[...], low, TN)
        total = term if total is None else total + term
    out_ref[...] = total[:share].astype(out_ref.dtype)
    rows = [piece[0:16, lanes - LANES :].astype(F32)[0:1] for piece in pieces]
    rows += [jnp.zeros((16 - len(rows), LANES), F32)]
    counts_ref[...] = jnp.concatenate(rows, axis=0).astype(BF16)


def join_kernel(mine_ref, got_ref, my_counts, got_counts, out_ref, counts_ref):
    out_ref[...] = (mine_ref[...] + got_ref[...].astype(F32)).astype(BF16)
    a, b = my_counts[...].astype(F32), got_counts[...].astype(F32)
    rows = [side[k : k + 1] for k in range(SEGMENT // 2) for side in (a, b)]
    counts_ref[...] = jnp.concatenate(rows, axis=0).astype(jnp.int32)


def query_kernel(f_ref, m0, m1, m2, m3, q_ref, v_ref, merged, sems):
    shard = m0.shape[0]
    width = 4 * shard // 3
    heads = width // HD
    phases = q_ref.shape[0]
    mine = lax.axis_index("col")
    copies = []
    for j, ref in enumerate((m0, m1, m2, m3)):
        spot = pl.multiple_of((mine ^ j) * shard, 64)
        copies.append(pltpu.make_async_copy(ref, merged.at[pl.ds(spot, shard)], sems.at[j]))
        copies[-1].start()
    f = f_ref[...].astype(F32).T.astype(BF16)
    bucket = f.shape[1] // phases
    for copy in copies:
        copy.wait()
    factor = math.log2(math.e) / math.sqrt(HD)
    rows = lax.broadcasted_iota(jnp.int32, (2 * HD, 1), 0)
    for pair in range(heads // 2):
        both = slice(pair * 2 * HD, (pair + 1) * 2 * HD)
        queries = dot(merged[both], f).astype(BF16).astype(F32)
        keys = merged[width + pair * 2 * HD : width + (pair + 1) * 2 * HD]
        for h in range(2):
            one = jnp.where(rows // HD == h, queries, 0.0).astype(BF16)
            wide = (dot(keys, one, TN) * factor).astype(BF16)
            for p in range(phases):
                q_ref[p, pair, :, h * bucket : (h + 1) * bucket] = wide[:, p * bucket : (p + 1) * bucket]
    v_ref[...] = merged[2 * width :]


def attend_kernel(spare, counts_ref, q_ref, v_ref, back_ref, *refs):
    around, across = refs[:4], refs[4:8]
    out_ref, rows32, keys, keys_t, mixed, good = refs[8:]
    phases, parts, channels, rows = q_ref.shape
    bucket = back_ref.shape[0] // phases
    tokens = phases * bucket
    group = SEGMENT * bucket
    few = group // 2
    pack = rows // bucket
    halves = range(channels // LANES)

    def part_of(j, p):
        step, side = j // 2, j % 2
        if side == 0:
            return around[step], p * bucket
        if step != 1 or 2 * p < phases:
            return across[step], p * bucket
        return around[2], tokens + (2 * p - phases) * bucket // 2

    fills = []
    for p in range(phases):
        filled = 0
        for j in range(SEGMENT):
            source, first = part_of(j, p)
            for c in halves:
                rows32[p, c, pl.ds(filled, bucket), :] = source[
                    first : first + bucket, c * LANES : (c + 1) * LANES
                ].astype(F32)
            filled = filled + counts_ref[j, spare + p]
        for c in halves:
            rows32[p, c, pl.ds(filled, few), :] = jnp.zeros((few, LANES), F32)
        fills.append(filled)
    most = functools.reduce(jnp.maximum, fills)

    def arrange(p, width):
        for c in halves:
            some = rows32[p, c, 0:width, :]
            keys[p, 0:width, c * LANES : (c + 1) * LANES] = some.astype(BF16)
            keys_t[p, c * LANES : (c + 1) * LANES, 0:width] = some.T.astype(BF16)

    def one_part(p, part, width, limit, shift):
        place = lax.broadcasted_iota(jnp.int32, (width, rows), 0)
        scores = dot(keys[p, 0:width, :], q_ref[p, part]) + jnp.where(place < limit, 0.0, -1e30)
        if shift:
            scores = scores - jnp.max(scores, axis=0, keepdims=True)
        weights = jnp.exp2(scores)
        total = jnp.sum(weights, axis=0, keepdims=True)
        mix = (dot(keys_t[p, :, 0:width], weights.astype(BF16)) * (1.0 / total)).astype(BF16)
        for h in range(pack):
            mixed[p, part * pack + h] = mix[:, h * bucket : (h + 1) * bucket]
        return total

    good[0] = 0

    @pl.when(most <= few)
    def _():
        least = greatest = None
        for p in range(phases):
            arrange(p, few)
            for part in range(parts):
                total = one_part(p, part, few, fills[p], False)
                least = total if least is None else jnp.minimum(least, total)
                greatest = total if greatest is None else jnp.maximum(greatest, total)
        inside = jnp.where((least >= 2.0**-60) & (greatest <= 2.0**100), 1.0, 0.0)
        good[0] = jnp.min(inside).astype(jnp.int32)

    @pl.when(good[0] == 0)
    def _():
        def again(i, carry):
            p, part = i // parts, lax.rem(i, parts)
            limit = fills[0]
            for k in range(1, phases):
                limit = jnp.where(p == k, fills[k], limit)

            @pl.when(part == 0)
            def _():
                @pl.when(limit < few)
                def _():
                    for c in halves:
                        rows32[p, c, few:group, :] = jnp.zeros((group - few, LANES), F32)

                arrange(p, group)

            one_part(p, part, group, limit, True)
            return carry

        lax.fori_loop(0, phases * parts, again, 0)

    outs = []
    for h in range(parts * pack):
        side = jnp.concatenate([mixed[p, h] for p in range(phases)], axis=1)
        outs.append(dot(v_ref[h * HD : (h + 1) * HD], side))
    spot = lax.broadcasted_iota(jnp.int32, (1, bucket), 1)
    live = jnp.concatenate(
        [jnp.where(spot < counts_ref[0, spare + p], 1.0, 0.0) for p in range(phases)], axis=1
    )
    ordered = jnp.where(live > 0.5, jnp.concatenate(outs, axis=0), 0.0).astype(BF16)
    out_ref[...] = dot(back_ref[...], ordered, NT).astype(BF16)


def local(feat_in, conv_weight, conv_bias, proj_weight, qkv_weight, tissue, phase):
    in_rows, in_cols, channels = feat_in.shape
    out_rows, out_cols = in_rows // 2, in_cols // 2
    tokens = out_rows * out_cols
    row_count, col_count = lax.axis_size("row"), lax.axis_size("col")
    depth, out_width = qkv_weight.shape
    width = out_width // 3
    heads = width // HD
    share = out_width // col_count

    weight_x = flip(conv_weight, "col", 2)
    weight_core = flip(conv_weight, "col", 1)
    weight_far = flip(weight_x, "col", 1)
    labels = (phase * 2 + 1 - tissue).astype(F32)
    left, z, sort, back = call(
        prepare_kernel,
        (
            jax.ShapeDtypeStruct((in_rows, channels), BF16),
            jax.ShapeDtypeStruct((2, out_rows, out_cols, 3 * channels), BF16),
            jax.ShapeDtypeStruct((tokens, tokens), BF16),
            jax.ShapeDtypeStruct((tokens, tokens), BF16),
        ),
        [VMEM] * 2,
        (VMEM,) * 4,
        [VMEM((in_rows, channels // LANES, in_cols + 8, LANES), F32)],
        (feat_in, labels),
        "prepare",
        24,
    )
    left = shifted(left, "col")
    up = shifted(jnp.concatenate([left[in_rows - 16 :], feat_in[in_rows - 1]], axis=0), "row")

    here = labels[None] == 2.0 * jnp.arange(PHASES, dtype=F32)[:, None, None]
    own_counts = jnp.sum(here.astype(F32), axis=(1, 2)).astype(BF16)
    qkv_mine = lax.dynamic_slice(
        qkv_weight, (0, lax.axis_index("col") * share), (depth, share)
    )
    lanes = -share % LANES
    if lanes < PHASES:
        lanes += LANES
    beside = jnp.broadcast_to(jnp.pad(own_counts, (0, lanes - PHASES))[None], (depth, lanes))
    qkv_mine = jnp.concatenate([qkv_mine, beside], axis=1)
    spare = share % LANES
    ordered = row_count != SEGMENT
    if ordered:
        whole = lax.all_gather(qkv_mine, "row", axis=0, tiled=True)
        pieces = list(whole.reshape(SEGMENT, width // SEGMENT, share + lanes))
        groups = [
            [s * SEGMENT + i for i in range(SEGMENT)] for s in range(row_count // SEGMENT)
        ]
        spot = lax.rem(lax.axis_index("row"), SEGMENT)
        y = lax.rem(spot, 2)
        order = jnp.stack([2 * z_from + side for z_from in behind(spot // 2) for side in (y, 1 - y)])
        counts = lax.all_gather(own_counts, "row", axis_index_groups=groups)[order]
        counts = jnp.pad(counts.astype(jnp.int32), ((0, 0), (spare, LANES - spare - PHASES)))
    else:
        pieces = [qkv_mine]
        for _ in range(3):
            pieces.append(ring(pieces[-1]))
        z, *pieces = lax.optimization_barrier((z, *pieces))

    mine = call(
        conv_kernel,
        jax.ShapeDtypeStruct((tokens, channels), BF16),
        [VMEM] + [ANY] * 4 + [VMEM] * 5,
        VMEM,
        [
            VMEM((9 * channels, channels), BF16),
            VMEM((2, channels // LANES, in_cols + 8, LANES), F32),
            pltpu.SemaphoreType.DMA((4,)),
        ],
        (
            z, conv_weight, weight_core, weight_x, weight_far, proj_weight, sort, left, up,
            conv_bias.reshape(1, channels),
        ),
        "conv",
        24,
    )

    half = tokens // 2
    around, across = [mine], []
    message = mine
    for step in range(4):
        passed = flip(message[:half] if step == 1 else message[:tokens], "row", 1)
        if step < 3:
            message, passed = lax.optimization_barrier((ring(message[:tokens] if step == 2 else message), passed))
            around.append(message)
        across.append(passed)
        if step == 0:
            message = jnp.concatenate([message, passed[half:]], axis=0)

    merged, counts_mine = call(
        functools.partial(merge_kernel, ordered),
        (
            jax.ShapeDtypeStruct((share, channels), BF16 if ordered else F32),
            jax.ShapeDtypeStruct((16, LANES), BF16),
        ),
        [VMEM] * (len(pieces) + 1),
        (VMEM, VMEM),
        [],
        (*pieces, proj_weight.T),
        "merge",
        16,
    )
    if not ordered:
        got = flip(jnp.concatenate([merged.astype(BF16), jnp.pad(counts_mine, ((0, 0), (0, channels - LANES)))], axis=0), "row", 1)
        merged, counts = call(
            join_kernel,
            (
                jax.ShapeDtypeStruct((share, channels), BF16),
                jax.ShapeDtypeStruct((SEGMENT, LANES), jnp.int32),
            ),
            [VMEM] * 4,
            (VMEM, VMEM),
            [],
            (merged, got[:share], counts_mine, got[share:, :LANES]),
            "join",
            16,
        )
    merged_x = flip(merged, "col", 2)
    merged_core = flip(merged, "col", 1)
    merged_far = flip(merged_x, "col", 1)
    bucket = tokens // PHASES
    queries, values = call(
        query_kernel,
        (
            jax.ShapeDtypeStruct((PHASES, heads // 2, channels, 2 * bucket), BF16),
            jax.ShapeDtypeStruct((width, channels), BF16),
        ),
        [VMEM, ANY, ANY, ANY, ANY],
        (VMEM, VMEM),
        [VMEM((out_width, channels), BF16), pltpu.SemaphoreType.DMA((4,))],
        (mine, merged, merged_core, merged_x, merged_far),
        "queries",
        24,
    )
    group = SEGMENT * bucket
    attended = call(
        functools.partial(attend_kernel, spare),
        jax.ShapeDtypeStruct((tokens, width), BF16),
        [pltpu.SMEM] + [VMEM] * (3 + SEGMENT),
        VMEM,
        [
            VMEM((PHASES, channels // LANES, group + group // 2, LANES), F32),
            VMEM((PHASES, group, channels), BF16),
            VMEM((PHASES, channels, group), BF16),
            VMEM((PHASES, heads, channels, bucket), BF16),
            pltpu.SMEM((1,), jnp.int32),
        ],
        (counts, queries, values, back, *around, *across),
        "attend",
        36,
    )
    return attended.reshape(out_rows, out_cols, width)


def solution(mesh):
    in_specs = (
        P("row", "col", None),
        P("col", None),
        P(),
        P(),
        P("row", None),
        P("row", "col"),
        P("row", "col"),
    )
    out_specs = P("row", "col", None)
    return jax.shard_map(local, mesh=mesh, in_specs=in_specs, out_specs=out_specs, check_vma=False)
```

```python
import functools
import math

import jax
import jax.numpy as jnp
from jax import lax
from jax.experimental import pallas as pl
from jax.experimental.pallas import tpu as pltpu
from jax.sharding import PartitionSpec as P

HD = 64
PHASES = 4
SEGMENT = 8
LANES = 128
BF16 = jnp.bfloat16
F32 = jnp.float32
NT = (((1,), (1,)), ((), ()))
TN = (((0,), (0,)), ((), ()))
VMEM = pltpu.VMEM
ANY = pl.ANY


def dot(a, b, dims=None):
    if dims is None:
        return jnp.dot(a, b, preferred_element_type=F32)
    return lax.dot_general(a, b, dims, preferred_element_type=F32)


def flip(array, axis, bits):
    return lax.ppermute(array, axis, [(i, i ^ bits) for i in range(lax.axis_size(axis))])


def shifted(array, axis):
    return lax.ppermute(array, axis, [(i, i + 1) for i in range(lax.axis_size(axis) - 1)])


HOPS = (1, 3, 0, 2)


def ring(array):
    pairs = []
    for i in range(lax.axis_size("row")):
        z, y = i % SEGMENT // 2, i % 2
        pairs.append((i, i // SEGMENT * SEGMENT + 2 * HOPS[z] + y))
    return lax.ppermute(array, "row", pairs)


def behind(z):
    found = [z]
    for _ in range(len(HOPS) - 1):
        z = found[-1]
        found.append(jnp.where(z == 0, 2, jnp.where(z == 1, 0, jnp.where(z == 2, 3, 1))))
    return found


def call(kernel, out_shape, in_spaces, out_spaces, scratch, args, name, mib):
    return pl.pallas_call(
        kernel,
        out_shape=out_shape,
        in_specs=[pl.BlockSpec(memory_space=s) for s in in_spaces],
        out_specs=(
            tuple(pl.BlockSpec(memory_space=s) for s in out_spaces)
            if isinstance(out_spaces, tuple)
            else pl.BlockSpec(memory_space=out_spaces)
        ),
        scratch_shapes=scratch,
        compiler_params=pltpu.CompilerParams(vmem_limit_bytes=mib * 1024 * 1024),
        cost_estimate=pl.CostEstimate(flops=0, bytes_accessed=0, transcendentals=0),
        name=name,
    )(*args)


def prepare_kernel(
    x_ref, label_ref, z_ref, sort_ref, back_ref, wide
):
    rows, cols, channels = x_ref.shape
    out_rows, out_cols = label_ref.shape
    half = cols // 2
    tokens = out_rows * out_cols
    bucket = tokens // PHASES
    def one_row(r, carry):
        for c in range(channels // LANES):
            wide[r, c, pl.ds(0, 8), :] = jnp.zeros((8, LANES), F32)
            wide[r, c, pl.ds(8, cols), :] = x_ref[r, :, c * LANES : (c + 1) * LANES].astype(F32)
            for b in range(3):
                spot = b * channels + c * LANES
                z_ref[r % 2, r // 2, :, spot : spot + LANES] = wide[
                    r, c, pl.ds(7 + b, half, stride=2), :
                ].astype(BF16)
        return carry

    lax.fori_loop(0, rows, one_row, 0, unroll=2)

    def iota(shape, axis):
        return lax.broadcasted_iota(jnp.int32, shape, axis)

    labels = label_ref[...].astype(BF16)
    spread = (iota((out_cols, tokens), 0) == lax.rem(iota((out_cols, tokens), 1), out_cols)).astype(F32)
    along = dot(labels, spread.astype(BF16))
    in_row = iota((out_rows, tokens), 0) == iota((out_rows, tokens), 1) // out_cols
    cls = jnp.sum(jnp.where(in_row, along, 0.0), axis=0, keepdims=True).astype(jnp.int32)
    classes = iota((16, tokens), 0)
    cls = jnp.broadcast_to(cls, (16, tokens))
    member = (classes == cls).astype(F32)
    earlier = (iota((tokens, tokens), 0) < iota((tokens, tokens), 1)).astype(F32)
    rank = dot(member.astype(BF16), earlier.astype(BF16))
    odd = lax.rem(classes, 2) == 1
    live_before = jnp.where(odd & (classes - 1 == cls), 1.0, 0.0)
    start = (classes // 2 * bucket).astype(F32) + jnp.sum(live_before, axis=1, keepdims=True)
    place = jnp.sum(member * (rank + start), axis=0, keepdims=True)
    place = jnp.broadcast_to(place, (LANES, tokens))
    sort_ref[...] = (
        iota((tokens, tokens), 0) == jnp.broadcast_to(place[0:1].astype(jnp.int32), (tokens, tokens))
    ).astype(F32).astype(BF16)
    column = place.T[:, 0:1].astype(jnp.int32)
    back_ref[...] = (iota((tokens, tokens), 1) == column).astype(F32).astype(BF16)


def conv_kernel(
    z_ref, packed_ref, w1, w2, w3, sort_ref, left_ref, up_ref, bias_ref,
    out_ref, weight, edge, sems,
):
    out_rows, out_cols, wide = z_ref.shape[1:]
    channels = wide // 3
    tokens = out_rows * out_cols
    shard = w1.shape[0]
    mine = lax.axis_index("col")
    copies = []
    for j, ref in enumerate((packed_ref.at[pl.ds(0, shard)], w1, w2, w3)):
        spot = pl.multiple_of((mine ^ j) * shard, 64)
        copies.append(pltpu.make_async_copy(ref, weight.at[pl.ds(spot, shard)], sems.at[j]))
    for copy in copies:
        copy.start()
    in_rows = left_ref.shape[0]
    corner = up_ref[0:16].astype(F32)
    halves = range(channels // LANES)
    for c in halves:
        few = slice(c * LANES, (c + 1) * LANES)
        edge[0, c, pl.ds(0, 8), :] = corner[8:16, few]
        edge[0, c, pl.ds(8, in_rows), :] = left_ref[:, few].astype(F32)
        edge[1, c, pl.ds(0, 8), :] = jnp.zeros((8, LANES), F32)
        edge[1, c, pl.ds(8, 2 * out_cols), :] = up_ref[16:, few].astype(F32)

    def every_second(side, first, count):
        parts = [edge[side, c, pl.ds(first, count, stride=2), :] for c in halves]
        return jnp.concatenate(parts, axis=1).astype(BF16)

    lefts = [every_second(0, 7 + a, out_rows) for a in range(3)]
    ups = [every_second(1, 7 + b, out_cols) for b in range(3)]
    for copy in copies:
        copy.wait()
    even = z_ref[0].reshape(tokens, wide)
    odd = z_ref[1].reshape(tokens, wide)
    acc = dot(even, weight[wide : 2 * wide]) + dot(odd, weight[2 * wide : 3 * wide])
    above = dot(odd[: tokens - out_cols], weight[:wide])
    top = dot(jnp.concatenate(ups, axis=1), weight[:wide])
    acc = acc + jnp.concatenate([top, above], axis=0)
    side = sum(dot(lefts[a], weight[a * wide : a * wide + channels]) for a in range(3))
    grid = acc.reshape(out_rows, out_cols, channels)
    first = lax.broadcasted_iota(jnp.int32, grid.shape, 1) == 0
    grid = grid + jnp.where(first, side[:, None, :], 0.0)
    pre = grid.reshape(tokens, channels) + bias_ref[...]
    features = jax.nn.gelu(pre).astype(BF16)
    projected = jnp.concatenate(
        [
            dot(features, packed_ref[at : at + channels])
            for at in range(shard, packed_ref.shape[0], channels)
        ],
        axis=1,
    )
    centred = projected - jnp.mean(projected, axis=1, keepdims=True)
    spread = jnp.mean(centred * centred, axis=1, keepdims=True)
    scaled = (features.astype(F32) * lax.rsqrt(spread + 1e-05)).astype(BF16)
    out_ref[...] = dot(sort_ref[...], scaled).astype(BF16)


def merge_kernel(ordered, *refs):
    pieces, (proj_ref, out_ref, counts_ref) = refs[:-3], refs[-3:]
    share = out_ref.shape[0]
    depth, lanes = pieces[0].shape
    mine = lax.rem(lax.axis_index("row"), SEGMENT)
    if ordered:
        order = range(SEGMENT)
    else:
        order = [2 * z + lax.rem(mine, 2) for z in behind(mine // 2)]
    mean = jnp.mean(proj_ref[...].astype(F32), axis=0, keepdims=True)
    total = None
    for piece, j in zip(pieces, order):
        spot = pl.multiple_of(j * depth, 32)
        part = proj_ref[pl.ds(spot, depth), :].astype(F32) - mean
        high = part.astype(BF16)
        low = (part - high.astype(F32)).astype(BF16)
        term = dot(piece[...], high, TN) + dot(piece[...], low, TN)
        total = term if total is None else total + term
    out_ref[...] = total[:share].astype(out_ref.dtype)
    rows = [piece[0:16, lanes - LANES :].astype(F32)[0:1] for piece in pieces]
    rows += [jnp.zeros((16 - len(rows), LANES), F32)]
    counts_ref[...] = jnp.concatenate(rows, axis=0).astype(BF16)


def join_kernel(mine_ref, got_ref, my_counts, got_counts, out_ref, counts_ref):
    out_ref[...] = (mine_ref[...] + got_ref[...].astype(F32)).astype(BF16)
    a, b = my_counts[...].astype(F32), got_counts[...].astype(F32)
    rows = [side[k : k + 1] for k in range(SEGMENT // 2) for side in (a, b)]
    counts_ref[...] = jnp.concatenate(rows, axis=0).astype(jnp.int32)


def query_kernel(f_ref, m0, m1, m2, m3, q_ref, v_ref, merged, sems):
    shard = m0.shape[0]
    width = 4 * shard // 3
    heads = width // HD
    phases = q_ref.shape[0]
    mine = lax.axis_index("col")
    copies = []
    for j, ref in enumerate((m0, m1, m2, m3)):
        spot = pl.multiple_of((mine ^ j) * shard, 64)
        copies.append(pltpu.make_async_copy(ref, merged.at[pl.ds(spot, shard)], sems.at[j]))
        copies[-1].start()
    f = f_ref[...].astype(F32).T.astype(BF16)
    bucket = f.shape[1] // phases
    for copy in copies:
        copy.wait()
    factor = math.log2(math.e) / math.sqrt(HD)
    rows = lax.broadcasted_iota(jnp.int32, (2 * HD, 1), 0)
    for pair in range(heads // 2):
        both = slice(pair * 2 * HD, (pair + 1) * 2 * HD)
        queries = dot(merged[both], f).astype(BF16).astype(F32)
        keys = merged[width + pair * 2 * HD : width + (pair + 1) * 2 * HD]
        for h in range(2):
            one = jnp.where(rows // HD == h, queries, 0.0).astype(BF16)
            wide = (dot(keys, one, TN) * factor).astype(BF16)
            for p in range(phases):
                q_ref[p, pair, :, h * bucket : (h + 1) * bucket] = wide[:, p * bucket : (p + 1) * bucket]
    v_ref[...] = merged[2 * width :]


def attend_kernel(spare, counts_ref, q_ref, v_ref, back_ref, *refs):
    around, across = refs[:4], refs[4:8]
    out_ref, rows32, keys, keys_t, mixed, good = refs[8:]
    phases, parts, channels, rows = q_ref.shape
    bucket = back_ref.shape[0] // phases
    tokens = phases * bucket
    group = SEGMENT * bucket
    few = group // 2
    pack = rows // bucket
    halves = range(channels // LANES)

    def part_of(j, p):
        step, side = j // 2, j % 2
        if side == 0:
            return around[step], p * bucket
        if step != 1 or 2 * p < phases:
            return across[step], p * bucket
        return around[2], tokens + (2 * p - phases) * bucket // 2

    fills = []
    for p in range(phases):
        filled = 0
        for j in range(SEGMENT):
            source, first = part_of(j, p)
            for c in halves:
                rows32[p, c, pl.ds(filled, bucket), :] = source[
                    first : first + bucket, c * LANES : (c + 1) * LANES
                ].astype(F32)
            filled = filled + counts_ref[j, spare + p]
        for c in halves:
            rows32[p, c, pl.ds(filled, few), :] = jnp.zeros((few, LANES), F32)
        fills.append(filled)
    most = functools.reduce(jnp.maximum, fills)

    def arrange(p, width):
        for c in halves:
            some = rows32[p, c, 0:width, :]
            keys[p, 0:width, c * LANES : (c + 1) * LANES] = some.astype(BF16)
            keys_t[p, c * LANES : (c + 1) * LANES, 0:width] = some.T.astype(BF16)

    def one_part(p, part, width, limit, shift):
        place = lax.broadcasted_iota(jnp.int32, (width, rows), 0)
        scores = dot(keys[p, 0:width, :], q_ref[p, part]) + jnp.where(place < limit, 0.0, -1e30)
        if shift:
            scores = scores - jnp.max(scores, axis=0, keepdims=True)
        weights = jnp.exp2(scores)
        total = jnp.sum(weights, axis=0, keepdims=True)
        mix = (dot(keys_t[p, :, 0:width], weights.astype(BF16)) * (1.0 / total)).astype(BF16)
        for h in range(pack):
            mixed[p, part * pack + h] = mix[:, h * bucket : (h + 1) * bucket]
        return total

    good[0] = 0

    @pl.when(most <= few)
    def _():
        least = greatest = None
        for p in range(phases):
            arrange(p, few)
            for part in range(parts):
                total = one_part(p, part, few, fills[p], False)
                least = total if least is None else jnp.minimum(least, total)
                greatest = total if greatest is None else jnp.maximum(greatest, total)
        inside = jnp.where((least >= 2.0**-60) & (greatest <= 2.0**100), 1.0, 0.0)
        good[0] = jnp.min(inside).astype(jnp.int32)

    @pl.when(good[0] == 0)
    def _():
        def again(i, carry):
            p, part = i // parts, lax.rem(i, parts)
            limit = fills[0]
            for k in range(1, phases):
                limit = jnp.where(p == k, fills[k], limit)

            @pl.when(part == 0)
            def _():
                @pl.when(limit < few)
                def _():
                    for c in halves:
                        rows32[p, c, few:group, :] = jnp.zeros((group - few, LANES), F32)

                arrange(p, group)

            one_part(p, part, group, limit, True)
            return carry

        lax.fori_loop(0, phases * parts, again, 0)

    outs = []
    for h in range(parts * pack):
        side = jnp.concatenate([mixed[p, h] for p in range(phases)], axis=1)
        outs.append(dot(v_ref[h * HD : (h + 1) * HD], side))
    spot = lax.broadcasted_iota(jnp.int32, (1, bucket), 1)
    live = jnp.concatenate(
        [jnp.where(spot < counts_ref[0, spare + p], 1.0, 0.0) for p in range(phases)], axis=1
    )
    ordered = jnp.where(live > 0.5, jnp.concatenate(outs, axis=0), 0.0).astype(BF16)
    out_ref[...] = dot(back_ref[...], ordered, NT).astype(BF16)


def local(feat_in, conv_weight, conv_bias, proj_weight, qkv_weight, tissue, phase):
    in_rows, in_cols, channels = feat_in.shape
    out_rows, out_cols = in_rows // 2, in_cols // 2
    tokens = out_rows * out_cols
    row_count, col_count = lax.axis_size("row"), lax.axis_size("col")
    depth, out_width = qkv_weight.shape
    width = out_width // 3
    heads = width // HD
    share = out_width // col_count

    weight_x = flip(conv_weight, "col", 2)
    weight_core = flip(conv_weight, "col", 1)
    weight_far = flip(weight_x, "col", 1)
    labels = (phase * 2 + 1 - tissue).astype(F32)
    z, sort, back = call(
        prepare_kernel,
        (
            jax.ShapeDtypeStruct((2, out_rows, out_cols, 3 * channels), BF16),
            jax.ShapeDtypeStruct((tokens, tokens), BF16),
            jax.ShapeDtypeStruct((tokens, tokens), BF16),
        ),
        [VMEM] * 2,
        (VMEM,) * 3,
        [VMEM((in_rows, channels // LANES, in_cols + 8, LANES), F32)],
        (feat_in, labels),
        "prepare",
        24,
    )
    left = shifted(feat_in[:, in_cols - 1], "col")
    up = shifted(jnp.concatenate([left[in_rows - 16 :], feat_in[in_rows - 1]], axis=0), "row")

    here = labels[None] == 2.0 * jnp.arange(PHASES, dtype=F32)[:, None, None]
    own_counts = jnp.sum(here.astype(F32), axis=(1, 2)).astype(BF16)
    qkv_mine = lax.dynamic_slice(
        qkv_weight, (0, lax.axis_index("col") * share), (depth, share)
    )
    lanes = -share % LANES
    if lanes < PHASES:
        lanes += LANES
    beside = jnp.broadcast_to(jnp.pad(own_counts, (0, lanes - PHASES))[None], (depth, lanes))
    qkv_mine = jnp.concatenate([qkv_mine, beside], axis=1)
    spare = share % LANES
    ordered = row_count != SEGMENT
    if ordered:
        whole = lax.all_gather(qkv_mine, "row", axis=0, tiled=True)
        pieces = list(whole.reshape(SEGMENT, width // SEGMENT, share + lanes))
        groups = [
            [s * SEGMENT + i for i in range(SEGMENT)] for s in range(row_count // SEGMENT)
        ]
        spot = lax.rem(lax.axis_index("row"), SEGMENT)
        y = lax.rem(spot, 2)
        order = jnp.stack([2 * z_from + side for z_from in behind(spot // 2) for side in (y, 1 - y)])
        counts = lax.all_gather(own_counts, "row", axis_index_groups=groups)[order]
        counts = jnp.pad(counts.astype(jnp.int32), ((0, 0), (spare, LANES - spare - PHASES)))
    else:
        pieces = [qkv_mine]
        for _ in range(3):
            pieces.append(ring(pieces[-1]))
        z, *pieces = lax.optimization_barrier((z, *pieces))

    blocks = range(0, width, channels)
    packed_weight = jnp.concatenate(
        [conv_weight] + [proj_weight[:, at : at + channels] for at in blocks], axis=0
    )
    mine = call(
        conv_kernel,
        jax.ShapeDtypeStruct((tokens, channels), BF16),
        [VMEM, VMEM] + [ANY] * 3 + [VMEM] * 4,
        VMEM,
        [
            VMEM((9 * channels, channels), BF16),
            VMEM((2, channels // LANES, in_cols + 8, LANES), F32),
            pltpu.SemaphoreType.DMA((4,)),
        ],
        (
            z, packed_weight, weight_core, weight_x, weight_far, sort, left, up,
            conv_bias.reshape(1, channels),
        ),
        "conv",
        24,
    )

    half = tokens // 2
    around, across = [mine], []
    message = mine
    for step in range(4):
        passed = flip(message[:half] if step == 1 else message[:tokens], "row", 1)
        if step < 3:
            message, passed = lax.optimization_barrier((ring(message[:tokens] if step == 2 else message), passed))
            around.append(message)
        across.append(passed)
        if step == 0:
            message = jnp.concatenate([message, passed[half:]], axis=0)

    merged, counts_mine = call(
        functools.partial(merge_kernel, ordered),
        (
            jax.ShapeDtypeStruct((share, channels), BF16 if ordered else F32),
            jax.ShapeDtypeStruct((16, LANES), BF16),
        ),
        [VMEM] * (len(pieces) + 1),
        (VMEM, VMEM),
        [],
        (*pieces, proj_weight.T),
        "merge",
        16,
    )
    if not ordered:
        got = flip(jnp.concatenate([merged.astype(BF16), jnp.pad(counts_mine, ((0, 0), (0, channels - LANES)))], axis=0), "row", 1)
        merged, counts = call(
            join_kernel,
            (
                jax.ShapeDtypeStruct((share, channels), BF16),
                jax.ShapeDtypeStruct((SEGMENT, LANES), jnp.int32),
            ),
            [VMEM] * 4,
            (VMEM, VMEM),
            [],
            (merged, got[:share], counts_mine, got[share:, :LANES]),
            "join",
            16,
        )
    merged_x = flip(merged, "col", 2)
    merged_core = flip(merged, "col", 1)
    merged_far = flip(merged_x, "col", 1)
    bucket = tokens // PHASES
    queries, values = call(
        query_kernel,
        (
            jax.ShapeDtypeStruct((PHASES, heads // 2, channels, 2 * bucket), BF16),
            jax.ShapeDtypeStruct((width, channels), BF16),
        ),
        [VMEM, ANY, ANY, ANY, ANY],
        (VMEM, VMEM),
        [VMEM((out_width, channels), BF16), pltpu.SemaphoreType.DMA((4,))],
        (mine, merged, merged_core, merged_x, merged_far),
        "queries",
        24,
    )
    group = SEGMENT * bucket
    attended = call(
        functools.partial(attend_kernel, spare),
        jax.ShapeDtypeStruct((tokens, width), BF16),
        [pltpu.SMEM] + [VMEM] * (3 + SEGMENT),
        VMEM,
        [
            VMEM((PHASES, channels // LANES, group + group // 2, LANES), F32),
            VMEM((PHASES, group, channels), BF16),
            VMEM((PHASES, channels, group), BF16),
            VMEM((PHASES, heads, channels, bucket), BF16),
            pltpu.SMEM((1,), jnp.int32),
        ],
        (counts, queries, values, back, *around, *across),
        "attend",
        36,
    )
    return attended.reshape(out_rows, out_cols, width)


def solution(mesh):
    in_specs = (
        P("row", "col", None),
        P("col", None),
        P(),
        P(),
        P("row", None),
        P("row", "col"),
        P("row", "col"),
    )
    out_specs = P("row", "col", None)
    return jax.shard_map(local, mesh=mesh, in_specs=in_specs, out_specs=out_specs, check_vma=False)
```
